128 devices in a mesh: event: 4 (over x), region: 32 (over z, y, core).
Axes of the slice: x: 4, y: 4, z: 4, core: 2. Of those that a mesh axis runs over, the one named last changes fastest.
Arguments:
- queries_in: bfloat16 [4096, 512], P('event'), parts along dimension 0, may hold values from -144 to 144
- hits_in: bfloat16 [131072, 512], P(('event', 'region')), parts along dimension 0, may hold values from -6 to 6
- w_query: bfloat16 [512, 512], replicated, may hold values from -0.25 to 0.25
- w_key: bfloat16 [512, 512], replicated, may hold values from -0.25 to 0.25
- w_value: bfloat16 [512, 512], replicated, may hold values from -0.25 to 0.25
- w_out: bfloat16 [512, 512], replicated, may hold values from -0.25 to 0.25
- mask_list: int32 [32, 64], P('event'), parts along dimension 0, may hold values from 0 to 255, all different within a row
- grad_out: bfloat16 [4096, 512], P('event'), parts along dimension 0, may hold values from -6 to 6
Outputs:
- layer_out: bfloat16 [4096, 512], P('event'), parts along dimension 0
- grad_queries: bfloat16 [4096, 512], P('event'), parts along dimension 0
- grad_hits: bfloat16 [131072, 512], P(('event', 'region')), parts along dimension 0
- grad_wq: float32 [2048, 512], P('event'), parts along dimension 0
- grad_wk: float32 [2048, 512], P('event'), parts along dimension 0
- grad_wv: float32 [2048, 512], P('event'), parts along dimension 0
- grad_wo: float32 [2048, 512], P('event'), parts along dimension 0
The draws below stay inside these ranges and needn't reach their ends.
There are 4 independent parts, one for each index of `event`. The reference program is written for one: setup_inputs(seed, part) draws one part's arguments, and reference() takes and returns one part's arrays. A program takes and returns all parts, laid end to end along the dimension named above; an argument that names none is the same for every part. Nothing has to cross between parts.
Inputs may be any that keep to these rules, and one draw needn't show every extreme that they name: `mask_list`: each row names 64 different hit blocks, and every hit block is named by some row.
All inputs are finite; a program needn't handle non-finite values.
Results may differ from the reference program's by a relative error of at most 0.04.
The reference program's roundings to bfloat16 on the way (of `attended`, `grad_att`, `grad_vals`, `grad_scores`, `grad_keys` and `grad_q`) count: a program that leaves them out, or rounds other values in their place, can miss the bound.
Values may be sent and summed in bfloat16 or wider, within the bound.
A program may use at most 192 MiB of HBM per device.

```python
import math
import jax
import jax.numpy as jnp
from jax import lax

D = 512
HEADS = 8
BLOCK = 128
QUERIES = 1024
HIT_DEV = 1024
HITS = 32768
HBLK_DEV = 8
NBLOCKS = 256
QBLOCKS = 8
LIST = 64
N_REGION = 32


def draw_queries_in(key, part):
    base = jnp.clip(jax.random.normal(key, (QUERIES, D), jnp.float32), -6.0, 6.0)
    return base.astype(jnp.bfloat16)


def levels(own_key, dims, cuts, low, largest):
    factor_of, own = 1.0, jax.random.fold_in(own_key, 6)
    for dim, blocks in cuts:
        heights = jnp.exp(jax.random.uniform(jax.random.fold_in(own, dim), (blocks,), jnp.float32, low / len(cuts), largest / len(cuts)))
        factor_of = factor_of * jnp.repeat(heights, dims[dim] // blocks).reshape([-1 if axis == dim else 1 for axis in range(len(dims))])
    return factor_of


def different_ones(own_key, rows, count, top, lift):
    ranking = jax.random.permutation(jax.random.fold_in(own_key, 1), count)
    boost = ranking
    for power in range(3):
        boost = boost * boost // count
    boost = boost * lift // count
    lots = jax.random.randint(jax.random.fold_in(own_key, 2), (rows, count), 0, 4096) + boost
    fixed_rows = jax.random.permutation(jax.random.fold_in(own_key, 3), rows)[jnp.arange(count) % rows]
    lots = jnp.where(jnp.arange(rows)[:, None] == fixed_rows[None, :], 1 << 14, lots)
    merit = lots * count + jnp.arange(count)
    return lax.top_k(merit.astype(jnp.int32), top)[1].astype(jnp.int32)


def gaussian(own_key, shape, deviation, reach, pieces=(), held_as=jnp.bfloat16):
    loudness = levels(own_key, shape, pieces, -0.22, 0.18) if pieces else 1.0
    values = jax.random.normal(own_key, shape, jnp.float32) * deviation * loudness
    return jnp.minimum(jnp.maximum(values, -reach), reach).astype(held_as)


def setup_inputs(seed: int = 0, part: int = 0) -> dict:
    key_of = jax.random.split(jax.random.key(seed), 9)
    part_splits = jax.random.split(jax.random.fold_in(key_of[8], part), 9)
    return {
        "queries_in": draw_queries_in(jax.random.fold_in(jax.random.fold_in(key_of[8], part), 71), part),
        "hits_in": gaussian(part_splits[1], (HITS, D), 1.0, 6.0, ((0, 32),)),
        "w_query": gaussian(key_of[2], (D, D), D ** -0.5, 0.25),
        "w_key": gaussian(key_of[3], (D, D), D ** -0.5, 0.25),
        "w_value": gaussian(key_of[4], (D, D), D ** -0.5, 0.25),
        "w_out": gaussian(key_of[5], (D, D), D ** -0.5, 0.25),
        "mask_list": different_ones(part_splits[6], QBLOCKS, NBLOCKS, LIST, 4096),
        "grad_out": gaussian(part_splits[7], (QUERIES, D), 1.0, 6.0),
    }


def split_heads(array):
    return array.reshape(array.shape[:-1] + (HEADS, array.shape[-1] // HEADS))

def combine_stack(numerators, maxima, totals):
    peak = lax.optimization_barrier(jnp.max(maxima, axis=0))
    weights = jnp.exp(maxima - peak[None])
    total = lax.optimization_barrier(jnp.sum(totals * weights, axis=0))
    head_dim = numerators.shape[-1] // maxima.shape[-1]
    numer = lax.optimization_barrier(jnp.sum(numerators * jnp.repeat(weights, head_dim, axis=-1), axis=0))
    return (numer, peak, total)

def reference(queries_in, hits_in, w_query, w_key, w_value, w_out, mask_list, grad_out):
    f32 = jnp.float32
    bf16 = jnp.bfloat16
    score_scale = 1.0 / math.sqrt(D // HEADS)
    blockmask = jnp.any(mask_list[:, :, None] == jnp.arange(NBLOCKS, dtype=jnp.int32)[None, None, :], axis=1)
    query = jnp.dot(queries_in, w_query, preferred_element_type=f32).astype(bf16)
    query_heads = split_heads(query).astype(f32)
    hits_split = hits_in.reshape(N_REGION, HIT_DEV, D)
    region_cols = jnp.transpose(blockmask.reshape(QBLOCKS, N_REGION, HBLK_DEV), (1, 0, 2))

    def project(hits_part):
        keys = jnp.dot(hits_part, w_key, preferred_element_type=f32).astype(bf16)
        vals = jnp.dot(hits_part, w_value, preferred_element_type=f32).astype(bf16)
        return (keys, vals)

    def full_mask(columns):
        return jnp.repeat(jnp.repeat(columns, BLOCK, axis=0), BLOCK, axis=1)[:, None, :]

    def region_scores(keys, allowed):
        return jnp.einsum('qhd,khd->qhk', query_heads, split_heads(keys).astype(f32)) * score_scale

    def forward_region(inputs):
        hits_part, columns = inputs
        keys, vals = project(hits_part)
        allowed = full_mask(columns)
        scores = region_scores(keys, allowed)
        masked = jnp.where(allowed, scores, -1e+30)
        maxima = lax.optimization_barrier(jnp.max(masked, axis=2))
        exponents = jnp.where(allowed, jnp.exp(masked - maxima[..., None]), 0.0)
        totals = lax.optimization_barrier(jnp.sum(exponents, axis=2))
        numer = jnp.einsum('qhk,khd->qhd', exponents.astype(bf16).astype(f32), split_heads(vals).astype(f32))
        return (numer.reshape(QUERIES, D), maxima, totals)
    numer_all, maxima_all, totals_all = lax.map(forward_region, (hits_split, region_cols))
    numer, peak, total = combine_stack(numer_all, maxima_all, totals_all)
    head_dim = D // HEADS
    attended = (numer / jnp.repeat(total, head_dim, axis=-1)).astype(bf16)
    log_total = peak + jnp.log(total)
    layer_out = (queries_in.astype(f32) + jnp.dot(attended, w_out, preferred_element_type=f32)).astype(bf16)
    grad_att = jnp.dot(grad_out, w_out.T, preferred_element_type=f32).astype(bf16)
    grad_wo = jnp.dot(attended.T, grad_out, preferred_element_type=f32)
    grad_heads = split_heads(grad_att).astype(f32)
    deltas = lax.optimization_barrier(jnp.sum(grad_heads * split_heads(attended).astype(f32), axis=2))

    def backward_region(running, inputs):
        hits_part, columns = inputs
        keys, vals = project(hits_part)
        allowed = full_mask(columns)
        scores = region_scores(keys, allowed)
        probs = jnp.where(allowed, jnp.exp(scores - log_total[..., None]), 0.0)
        grad_vals = jnp.einsum('qhk,qhd->khd', probs.astype(bf16).astype(f32), grad_heads)
        grad_probs = jnp.einsum('qhd,khd->qhk', grad_heads, split_heads(vals).astype(f32))
        grad_scores = (probs * (grad_probs - deltas[..., None]) * score_scale).astype(bf16).astype(f32)
        grad_q = jnp.einsum('qhk,khd->qhd', grad_scores, split_heads(keys).astype(f32)).reshape(QUERIES, D)
        grad_keys = jnp.einsum('qhk,qhd->khd', grad_scores, query_heads)
        return (running + grad_q, (grad_keys.reshape(HIT_DEV, D).astype(bf16), grad_vals.reshape(HIT_DEV, D).astype(bf16)))
    grad_q_sum, (keys_grad, vals_grad) = lax.scan(backward_region, jnp.zeros((QUERIES, D), f32), (hits_split, region_cols))
    grad_q = grad_q_sum.astype(bf16)
    keys_grad = keys_grad.reshape(HITS, D)
    vals_grad = vals_grad.reshape(HITS, D)
    grad_wq = jnp.dot(queries_in.T, grad_q, preferred_element_type=f32)
    grad_wk = jnp.dot(hits_in.T, keys_grad, preferred_element_type=f32)
    grad_wv = jnp.dot(hits_in.T, vals_grad, preferred_element_type=f32)
    grad_queries = (grad_out.astype(f32) + jnp.dot(grad_q, w_query.T, preferred_element_type=f32)).astype(bf16)
    grad_hits = (jnp.dot(keys_grad, w_key.T, preferred_element_type=f32) + jnp.dot(vals_grad, w_value.T, preferred_element_type=f32)).astype(bf16)
    return (layer_out, grad_queries, grad_hits, grad_wq, grad_wk, grad_wv, grad_wo)
```

```python
import jax
import jax.numpy as jnp
from jax import lax
from jax.experimental import pallas as pl
from jax.experimental.pallas import tpu as pltpu
from jax.sharding import PartitionSpec as P

f32 = jnp.float32
bf16 = jnp.bfloat16
HEADS = 8
PAIRS = 4
B = 128
QB = 8
HB = 8
D = 512
N = 1024
SCALE = 0.125
NEG = -1e30
VMEM_LIMIT = 60 * 1024 * 1024
MESH = pl.DeviceIdType.MESH
NN = (((1,), (0,)), ((), ()))
NT = (((1,), (1,)), ((), ()))
TN = (((0,), (0,)), ((), ()))


def dot(a, b, dims=NN):
    return lax.dot_general(a, b, dims, preferred_element_type=f32)


def transposed(block):
    return block.astype(f32).T.astype(block.dtype)


def pair_cols(p):
    return slice(p * B, (p + 1) * B)


def block_rows(i):
    return pl.ds(pl.multiple_of(i * B, B), B)


def read_mask(mask_ref, bits):
    first = lax.axis_index("region") * HB
    slot = mask_ref[...] - first
    inside = (slot >= 0) & (slot < HB)
    weight = jnp.where(inside, jnp.left_shift(1, jnp.clip(slot, 0, HB - 1)), 0).astype(f32)
    for qb in range(QB):
        bits[qb] = jnp.sum(weight[qb : qb + 1, :]).astype(jnp.int32)


def listed(bits, qb, hb):
    return (jnp.right_shift(bits[qb], hb) & 1) == 1


def lane_masks():
    lane = lax.broadcasted_iota(jnp.int32, (1, B), 1)
    even = jnp.where(lane < 64, 1.0, 0.0)
    return even.astype(bf16), (1.0 - even).astype(bf16)


def spread_heads(rows, p, out, masks):
    block = rows[:, pair_cols(p)]
    out[p, :B] = block * masks[0]
    out[p, B:] = block * masks[1]


def forward_kernel(queries, hits, w_query, w_key, w_value, mask_ref,
                   q_out, k_out, v_out, kt_out, even_out, odd_out,
                   vt, scores, heads_q, acc, peak, total, bits):
    read_mask(mask_ref, bits)
    masks = lane_masks()

    def project(i, _):
        rows = block_rows(i)
        k = dot(hits[rows, :], w_key[...]).astype(bf16)
        v = dot(hits[rows, :], w_value[...]).astype(bf16)
        k_out[rows, :] = k
        v_out[rows, :] = v
        kt_out[i] = transposed(k)
        vt[i] = transposed(v)
        q_out[rows, :] = (dot(queries[rows, :], w_query[...]) * SCALE).astype(bf16)
        return 0

    lax.fori_loop(0, 8, project, 0)

    def query_block(qb, _):
        rows = q_out[block_rows(qb), :]
        for p in range(PAIRS):
            spread_heads(rows, p, heads_q, masks)
        peak[...] = jnp.full(peak.shape, NEG, f32)
        total[...] = jnp.zeros(total.shape, f32)
        acc[...] = jnp.zeros(acc.shape, f32)

        def score_block(hb, _):
            @pl.when(listed(bits, qb, hb))
            def _():
                for p in range(PAIRS):
                    s = dot(k_out[block_rows(hb), pair_cols(p)], heads_q[p], NT)
                    scores[hb, p] = s
                    peak[p] = jnp.maximum(peak[p], jnp.max(s, axis=0, keepdims=True))

            return 0

        lax.fori_loop(0, HB, score_block, 0)

        def value_block(hb, _):
            @pl.when(listed(bits, qb, hb))
            def _():
                for p in range(PAIRS):
                    e = jnp.exp(scores[hb, p] - peak[p])
                    total[p] = total[p] + jnp.sum(e, axis=0, keepdims=True)
                    n = dot(vt[hb, pair_cols(p), :], e.astype(bf16))
                    acc[p, :64] = acc[p, :64] + n[:64, :B]
                    acc[p, 64:] = acc[p, 64:] + n[64:, B:]

            return 0

        lax.fori_loop(0, HB, value_block, 0)
        core, z = qb // 4, lax.rem(qb, 4)
        for p in range(PAIRS):
            for half, out in enumerate((even_out.at[core, p, z], odd_out.at[core, z, p])):
                lanes = slice(half * B, (half + 1) * B)
                out[:64] = acc[p, half * 64 : half * 64 + 64]
                out[64:72] = jnp.concatenate(
                    [peak[p, :, lanes], total[p, :, lanes], jnp.zeros((6, B), f32)], axis=0
                )
        return 0

    lax.fori_loop(0, QB, query_block, 0)


def place():
    r = lax.axis_index("region")
    return r // 8, lax.rem(r // 2, 4), lax.rem(r, 2)


def index_of(z, y, core):
    return (z * 4 + y) * 2 + core


def remote(src, dst, send, recv, peer):
    return pltpu.make_async_remote_copy(
        src_ref=src, dst_ref=dst, send_sem=send, recv_sem=recv,
        device_id={"region": peer}, device_id_type=MESH,
    )


def greet(peers):
    barrier = pltpu.get_barrier_semaphore()
    for peer in peers:
        pl.semaphore_signal(barrier, inc=1, device_id={"region": peer}, device_id_type=MESH)
    pl.semaphore_wait(barrier, len(peers))


def merge(parts):
    peak = parts[0][:, 64:65]
    for part in parts[1:]:
        peak = jnp.maximum(peak, part[:, 64:65])
    numer = total = None
    for part in parts:
        weight = jnp.exp(part[:, 64:65] - peak)
        n, t = part[:, :64] * weight, part[:, 65:66] * weight
        numer, total = (n, t) if numer is None else (numer + n, total + t)
    return numer, peak, total


def store_merged(ref, parts):
    numer, peak, total = merge(parts)
    ref[:, :64] = numer
    ref[:, 64:65] = peak
    ref[:, 65:66] = total


def softmax_kernel(even_in, odd_in, grad_out, w_out,
                   stats, gatt, attended,
                   pair_e, pair_o, half_e, half_o, first_e, first_o, quarter_e, quarter_o, second_e, second_o,
                   send, recv):
    z, y, core = place()
    sibling = index_of(z, y, 1 - core)
    ys = [lax.rem(y + i, 4) for i in (1, 2, 3)]
    zs = [lax.rem(z + i, 4) for i in (1, 2, 3)]
    y_peers = [index_of(z, v, core) for v in ys]
    z_peers = [index_of(v, y, core) for v in zs]
    cross = [index_of(z, v, 1 - core) for v in ys]
    greet([sibling] + y_peers + z_peers + cross)

    pair = [
        remote(src.at[1 - core], dst, send.at[i], recv.at[i], sibling)
        for i, (src, dst) in enumerate(((even_in, pair_e), (odd_in, pair_o)))
    ]
    for c in pair:
        c.start()

    def grad_att(i, _):
        rows = block_rows(i)
        gatt[rows, :] = dot(grad_out[rows, :], w_out[...], NT).astype(bf16)
        return 0

    lax.fori_loop(0, 8, grad_att, 0)

    stage1 = []
    for c, src, got, half, first, coords, peers, base in (
        (pair[0], even_in, pair_e, half_e, first_e, ys, y_peers, 2),
        (pair[1], odd_in, pair_o, half_o, first_o, zs, z_peers, 5),
    ):
        c.wait_recv()
        for j in range(4):
            store_merged(half.at[j], [src[core, j], got[j]])
        for i in range(3):
            d = remote(half.at[coords[i]], first.at[2 - i], send.at[base + i], recv.at[base + 2 - i], peers[i])
            d.start()
            stage1.append(d)
    stage2 = []
    for own, half, first, quarter, second, coords, peers, base, got in (
        (y, half_e, first_e, quarter_e, second_e, zs, z_peers, 8, 2),
        (z, half_o, first_o, quarter_o, second_o, ys, y_peers, 11, 5),
    ):
        for i in range(3):
            remote(first.at[i], first.at[i], send.at[got + i], recv.at[got + i], peers[i]).wait_recv()
        store_merged(quarter, [half[own], first[0], first[1], first[2]])
        for i in range(3):
            d = remote(quarter.at[coords[i]], second.at[2 - i], send.at[base + i], recv.at[base + 2 - i], peers[i])
            d.start()
            stage2.append(d)
    grads = gatt[block_rows(core * 4 + z), pl.ds(pl.multiple_of(y * B, B), B)].astype(f32).T
    tile = []
    logs, deltas = [], []
    for half, (own, quarter, second, got) in enumerate(
        ((z, quarter_e, second_e, 8), (y, quarter_o, second_o, 11))
    ):
        for i in range(3):
            remote(second.at[i], second.at[i], send.at[got + i], recv.at[got + i], sibling).wait_recv()
        numer, peak, total = merge([quarter[own][None], second[0:1], second[1:2], second[2:3]])
        att = (numer[0] / total[0]).astype(bf16).astype(f32)
        tile.append(att)
        logs.append(peak[0] + jnp.log(total[0]))
        deltas.append(jnp.sum(att * grads[half * 64 : half * 64 + 64], axis=0, keepdims=True))
    stats[z, y, core] = jnp.concatenate(logs + deltas + [jnp.zeros((4, B), f32)], axis=0)
    out = []
    mine = stats.at[z, y, core]
    for i, peer in enumerate([sibling] + y_peers + cross):
        slot = 0 if i == 0 else (3 - (i - 1) % 3) + (3 if i > 3 else 0)
        d = remote(mine, mine, send.at[14 + i], recv.at[14 + slot], peer)
        d.start()
        out.append(d)
    attended[...] = jnp.concatenate(tile, axis=0).T.astype(bf16)
    for i, (v, c) in enumerate([(y, 1 - core)] + [(v, core) for v in ys] + [(v, 1 - core) for v in ys]):
        there = stats.at[z, v, c]
        remote(there, there, send.at[14 + i], recv.at[14 + i], sibling).wait_recv()
    for i in range(3):
        d = remote(stats.at[z], stats.at[z], send.at[21 + i], recv.at[21 + 2 - i], z_peers[i])
        d.start()
        out.append(d)
    for i in range(3):
        there = stats.at[zs[i]]
        remote(there, there, send.at[21 + i], recv.at[21 + i], z_peers[i]).wait_recv()
    for d in pair + stage1 + stage2 + out:
        d.wait_send()


def backward_kernel(q, k, v, kt, gatt, stats, hits, w_key, w_value, mask_ref,
                    even_out, odd_out, grad_hits,
                    dk, dv, dkb, dvb, heads_q, heads_g, acc, bits):
    read_mask(mask_ref, bits)
    masks = lane_masks()
    dk[...] = jnp.zeros(dk.shape, f32)
    dv[...] = jnp.zeros(dv.shape, f32)

    def query_block(qb, _):
        core, z = qb // 4, lax.rem(qb, 4)
        rows, grads = q[block_rows(qb), :], gatt[block_rows(qb), :]
        for p in range(PAIRS):
            spread_heads(rows, p, heads_q, masks)
            spread_heads(grads, p, heads_g, masks)
        acc[...] = jnp.zeros(acc.shape, f32)

        def hit_block(hb, _):
            @pl.when(listed(bits, qb, hb))
            def _():
                here = block_rows(hb)
                for p in range(PAIRS):
                    cols = pair_cols(p)
                    stat = stats[z, p, core]
                    log_total = jnp.concatenate([stat[0:1], stat[1:2]], axis=1)
                    delta = jnp.concatenate([stat[2:3], stat[3:4]], axis=1)
                    s = dot(k[here, cols], heads_q[p], NT)
                    probs = jnp.exp(s - log_total)
                    dv[here, cols] += dot(probs.astype(bf16), heads_g[p])
                    dp = dot(v[here, cols], heads_g[p], NT)
                    ds = (probs * (dp - delta)).astype(bf16)
                    dk[here, cols] += dot(ds, heads_q[p])
                    n = dot(kt[hb, cols, :], ds)
                    acc[p, :64] = acc[p, :64] + n[:64, :B]
                    acc[p, 64:] = acc[p, 64:] + n[64:, B:]

            return 0

        lax.fori_loop(0, HB, hit_block, 0)
        for p in range(PAIRS):
            even_out[core, p, z, :64] = (acc[p, :64] * SCALE).astype(bf16)
            odd_out[core, z, p, :64] = (acc[p, 64:] * SCALE).astype(bf16)
        return 0

    lax.fori_loop(0, QB, query_block, 0)

    def finish(i, _):
        rows = block_rows(i)
        a, b = dk[rows, :].astype(bf16), dv[rows, :].astype(bf16)
        dkb[rows, :] = a
        dvb[rows, :] = b
        grad_hits[rows, :] = (dot(a, w_key[...], NT) + dot(b, w_value[...], NT)).astype(bf16)
        return 0

    lax.fori_loop(0, 8, finish, 0)
    for which, grad in enumerate((dkb, dvb)):
        for z in range(4):
            part = dot(hits[:, z * B : (z + 1) * B], grad[...], TN).astype(bf16)
            for p in range(PAIRS):
                even_out[which, p, z, 64:] = part[:64, pair_cols(p)]
                odd_out[which, z, p, 64:] = part[64:, pair_cols(p)]


def total_kernel(even_in, odd_in, attended,
                 gath_a, gath_b,
                 pair_e, pair_o, half_e, half_o, first_e, first_o, quarter_e, quarter_o, second_e, second_o,
                 send, recv):
    z, y, core = place()
    sibling = index_of(z, y, 1 - core)
    ys = [lax.rem(y + i, 4) for i in (1, 2, 3)]
    zs = [lax.rem(z + i, 4) for i in (1, 2, 3)]
    y_peers = [index_of(z, v, core) for v in ys]
    z_peers = [index_of(v, y, core) for v in zs]
    greet([sibling] + y_peers + z_peers)
    sent = []

    def go(src, dst, s, r, peer):
        d = remote(src, dst, send.at[s], recv.at[r], peer)
        d.start()
        sent.append(d)

    def got(ref, r):
        remote(ref, ref, send.at[r], recv.at[r], sibling).wait_recv()

    for i, (src, dst) in enumerate(((even_in, pair_e), (odd_in, pair_o))):
        go(src.at[1 - core], dst, i, i, sibling)
    for src, pair, half, first, coords, peers, base, i0 in (
        (even_in, pair_e, half_e, first_e, ys, y_peers, 2, 0),
        (odd_in, pair_o, half_o, first_o, zs, z_peers, 5, 1),
    ):
        got(pair, i0)
        for j in range(4):
            half[j] = (src[core, j].astype(f32) + pair[j].astype(f32)).astype(bf16)
        for i in range(3):
            go(half.at[coords[i]], first.at[2 - i], base + i, base + 2 - i, peers[i])
    for own, half, first, quarter, second, coords, peers, base, before in (
        (y, half_e, first_e, quarter_e, second_e, zs, z_peers, 8, 2),
        (z, half_o, first_o, quarter_o, second_o, ys, y_peers, 11, 5),
    ):
        for i in range(3):
            got(first.at[i], before + i)
        total = half[own].astype(f32)
        for i in range(3):
            total = total + first[i].astype(f32)
        quarter[...] = total.astype(bf16)
        for i in range(3):
            go(quarter.at[coords[i]], second.at[2 - i], base + i, base + 2 - i, peers[i])
    sums = []
    for own, quarter, second, before in ((z, quarter_e, second_e, 8), (y, quarter_o, second_o, 11)):
        for i in range(3):
            got(second.at[i], before + i)
        total = quarter[own].astype(f32)
        for i in range(3):
            total = total + second[i].astype(f32)
        sums.append(total)
    grad_q = jnp.concatenate([sums[0][:64], sums[1][:64]], axis=0).T.astype(bf16)
    att = attended[...]
    blocks = []
    for half, gath in enumerate((gath_a.at[core, z, y], gath_b.at[core, y, z])):
        rows = slice(half * 64, half * 64 + 64)
        gath[:64] = grad_q[rows]
        gath[64:128] = sums[half][64:].astype(bf16)
        gath[128:] = att[rows]
        blocks.append(gath)
    for i in range(3):
        go(blocks[0], blocks[0], 14 + i, 14 + 2 - i, y_peers[i])
        go(blocks[1], blocks[1], 17 + i, 17 + 2 - i, z_peers[i])
    for i in range(3):
        got(gath_a.at[core, z, ys[i]], 14 + i)
        got(gath_b.at[core, y, zs[i]], 17 + i)
    for i in range(3):
        go(gath_a.at[core, z], gath_a.at[core, z], 20 + i, 20 + 2 - i, z_peers[i])
        go(gath_b.at[core, y], gath_b.at[core, y], 23 + i, 23 + 2 - i, y_peers[i])
    go(gath_a.at[core, z], gath_a.at[core, z], 26, 26, sibling)
    go(gath_b.at[core, y], gath_b.at[core, y], 27, 27, sibling)
    for i in range(3):
        got(gath_a.at[core, zs[i]], 20 + i)
        go(gath_a.at[core, zs[i]], gath_a.at[core, zs[i]], 28 + i, 28 + i, sibling)
        got(gath_b.at[core, ys[i]], 23 + i)
        go(gath_b.at[core, ys[i]], gath_b.at[core, ys[i]], 31 + i, 31 + i, sibling)
    got(gath_a.at[1 - core, z], 26)
    got(gath_b.at[1 - core, y], 27)
    for i in range(3):
        got(gath_a.at[1 - core, zs[i]], 28 + i)
        got(gath_b.at[1 - core, ys[i]], 31 + i)
    for d in sent:
        d.wait_send()


def final_kernel(queries, grad_out, w_query, w_out, gath_a, gath_b,
                 layer_out, grad_queries, grad_wq, grad_wk, grad_wv, grad_wo,
                 grad_q, attended):
    for qb in range(QB):
        core, z = qb // 4, qb % 4
        for p in range(PAIRS):
            for half in range(2):
                block = gath_a.at[core, z, p] if half == 0 else gath_b.at[core, p, z]
                rows = slice(qb * B + half * 64, qb * B + half * 64 + 64)
                grad_q[rows, pair_cols(p)] = block[:64]
                attended[rows, pair_cols(p)] = block[128:]
                out = grad_wk if core == 0 else grad_wv
                local = slice(z * B + half * 64, z * B + half * 64 + 64)
                out[local, pair_cols(p)] = block[64:128].astype(f32)

    def rows_block(i, _):
        rows = block_rows(i)
        layer_out[rows, :] = (queries[rows, :].astype(f32) + dot(attended[rows, :], w_out[...])).astype(bf16)
        grad_queries[rows, :] = (grad_out[rows, :].astype(f32) + dot(grad_q[rows, :], w_query[...], NT)).astype(bf16)
        return 0

    lax.fori_loop(0, 8, rows_block, 0)
    for j in range(4):
        cols = pair_cols(j)
        grad_wq[cols, :] = dot(queries[:, cols], grad_q[...], TN)
        grad_wo[cols, :] = dot(attended[:, cols], grad_out[...], TN)


def shaped(*shape, dtype=f32):
    return jax.ShapeDtypeStruct(shape, dtype)


def call(kernel, args, outs, scratch, collective=None):
    in_vmem = pl.BlockSpec(memory_space=pltpu.VMEM)
    params = {"vmem_limit_bytes": VMEM_LIMIT}
    if collective is not None:
        params |= {"collective_id": collective, "has_side_effects": True}
    return pl.pallas_call(
        kernel,
        out_shape=outs,
        in_specs=[in_vmem] * len(args),
        out_specs=tuple([in_vmem] * len(outs)),
        scratch_shapes=scratch,
        compiler_params=pltpu.CompilerParams(**params),
        name=kernel.__name__,
    )(*args)


def stages(rows, dtype):
    shapes = []
    for lead in ((4, 4), (4, 4), (3, 4), (4,), (3,)):
        shapes += [pltpu.VMEM(lead + (rows, B), dtype)] * 2
    return shapes


def on_device(queries_in, hits_in, w_query, w_key, w_value, w_out, mask_list, grad_out):
    q, k, v, kt, even, odd = call(
        forward_kernel,
        (queries_in, hits_in, w_query, w_key, w_value, mask_list),
        (
            shaped(N, D, dtype=bf16), shaped(N, D, dtype=bf16), shaped(N, D, dtype=bf16),
            shaped(HB, D, B, dtype=bf16), shaped(2, 4, 4, 72, B), shaped(2, 4, 4, 72, B),
        ),
        [
            pltpu.VMEM((HB, D, B), bf16),
            pltpu.VMEM((HB, PAIRS, B, 2 * B), f32),
            pltpu.VMEM((PAIRS, 2 * B, B), bf16),
            pltpu.VMEM((PAIRS, B, B), f32),
            pltpu.VMEM((PAIRS, 1, 2 * B), f32),
            pltpu.VMEM((PAIRS, 1, 2 * B), f32),
            pltpu.SMEM((QB,), jnp.int32),
        ],
    )
    stats, gatt, attended = call(
        softmax_kernel,
        (even, odd, grad_out, w_out),
        (shaped(4, 4, 2, 8, B), shaped(N, D, dtype=bf16), shaped(B, B, dtype=bf16)),
        stages(72, f32) + [pltpu.SemaphoreType.DMA((24,)), pltpu.SemaphoreType.DMA((24,))],
        collective=0,
    )
    even, odd, grad_hits = call(
        backward_kernel,
        (q, k, v, kt, gatt, stats, hits_in, w_key, w_value, mask_list),
        (shaped(2, 4, 4, B, B, dtype=bf16), shaped(2, 4, 4, B, B, dtype=bf16), shaped(N, D, dtype=bf16)),
        [
            pltpu.VMEM((N, D), f32), pltpu.VMEM((N, D), f32),
            pltpu.VMEM((N, D), bf16), pltpu.VMEM((N, D), bf16),
            pltpu.VMEM((PAIRS, 2 * B, B), bf16), pltpu.VMEM((PAIRS, 2 * B, B), bf16),
            pltpu.VMEM((PAIRS, B, B), f32),
            pltpu.SMEM((QB,), jnp.int32),
        ],
    )
    gath_a, gath_b = call(
        total_kernel,
        (even, odd, attended),
        (shaped(2, 4, 4, 192, B, dtype=bf16), shaped(2, 4, 4, 192, B, dtype=bf16)),
        stages(B, bf16) + [pltpu.SemaphoreType.DMA((34,)), pltpu.SemaphoreType.DMA((34,))],
        collective=1,
    )
    layer_out, grad_queries, grad_wq, grad_wk, grad_wv, grad_wo = call(
        final_kernel,
        (queries_in, grad_out, w_query, w_out, gath_a, gath_b),
        (
            shaped(N, D, dtype=bf16), shaped(N, D, dtype=bf16),
            shaped(D, D), shaped(D, D), shaped(D, D), shaped(D, D),
        ),
        [pltpu.VMEM((N, D), bf16), pltpu.VMEM((N, D), bf16)],
    )
    return (layer_out, grad_queries, grad_hits, grad_wq, grad_wk, grad_wv, grad_wo)


def solution(mesh):
    per_event = P("event", None)
    per_region = P(("event", "region"), None)
    return jax.shard_map(
        on_device,
        mesh=mesh,
        in_specs=(per_event, per_region, P(), P(), P(), P(), per_event, per_event),
        out_specs=(per_event, per_event, per_region, per_event, per_event, per_event, per_event),
        check_vma=False,
    )
```

```python
import jax
import jax.numpy as jnp
from jax import lax
from jax.experimental import pallas as pl
from jax.experimental.pallas import tpu as pltpu
from jax.sharding import PartitionSpec as P

f32 = jnp.float32
bf16 = jnp.bfloat16
HEADS = 8
PAIRS = 4
B = 128
QB = 8
HB = 8
D = 512
N = 1024
SCALE = 0.125
NEG = -1e30
VMEM_LIMIT = 60 * 1024 * 1024
MESH = pl.DeviceIdType.MESH
NN = (((1,), (0,)), ((), ()))
NT = (((1,), (1,)), ((), ()))
TN = (((0,), (0,)), ((), ()))


def dot(a, b, dims=NN):
    return lax.dot_general(a, b, dims, preferred_element_type=f32)


def transposed(block):
    return block.astype(f32).T.astype(block.dtype)


def pair_cols(p):
    return slice(p * B, (p + 1) * B)


def block_rows(i):
    return pl.ds(pl.multiple_of(i * B, B), B)


def list_blocks(mask_ref, lists, counts):
    first = lax.axis_index("region") * HB
    slot = mask_ref[...] - first
    inside = (slot >= 0) & (slot < HB)
    weight = jnp.where(inside, jnp.left_shift(1, jnp.clip(slot, 0, HB - 1)), 0).astype(f32)
    for qb in range(QB):
        bits = jnp.sum(weight[qb : qb + 1, :]).astype(jnp.int32)
        count = jnp.int32(0)
        for hb in range(HB):
            lists[qb, count] = hb
            count = count + (jnp.right_shift(bits, hb) & 1)
        counts[qb] = count


def over_listed(lists, counts, qb, body):
    count = counts[qb]

    def two(i, _):
        body([lists[qb, 2 * i], lists[qb, 2 * i + 1]])
        return 0

    lax.fori_loop(0, count // 2, two, 0)

    @pl.when(lax.rem(count, 2) == 1)
    def _():
        body([lists[qb, count - 1]])


def gathered_rows(ref, blocks, cols):
    return jnp.concatenate([ref[block_rows(b), cols] for b in blocks], axis=0)


def gathered_cols(ref, blocks, rows):
    return jnp.concatenate([ref[b, rows, :] for b in blocks], axis=1)


def lane_masks():
    lane = lax.broadcasted_iota(jnp.int32, (1, B), 1)
    even = jnp.where(lane < 64, 1.0, 0.0)
    return even.astype(bf16), (1.0 - even).astype(bf16)


def spread_heads(rows, p, out, masks):
    block = rows[:, pair_cols(p)]
    out[p, :B] = block * masks[0]
    out[p, B:] = block * masks[1]


def loads(pairs, sems):
    copies = [pltpu.make_async_copy(src, dst, sems.at[i]) for i, (src, dst) in enumerate(pairs)]
    for c in copies:
        c.start()
    return copies


def forward_kernel(queries_h, hits_h, w_query_h, w_key_h, w_value_h, grad_out_h, w_out_h, mask_ref,
                   q_h, k_h, v_h, natt_e, natt_o, stats,
                   queries, hits, w_query, w_key, w_value, grad_out, w_out, q, k, v,
                   vt, gatt_t, heads_q, acc, peak, total, lists, counts, sems_in, sems_out):
    ins = loads(
        ((hits_h, hits), (w_value_h, w_value), (w_key_h, w_key), (queries_h, queries),
         (w_query_h, w_query), (grad_out_h, grad_out), (w_out_h, w_out)), sems_in)
    list_blocks(mask_ref, lists, counts)
    masks = lane_masks()
    outs = []

    def project(src, weight, out, scale=None):
        def part(i, _):
            rows = pl.ds(pl.multiple_of(i * 256, 256), 256)
            x = dot(src[rows, :], weight[...])
            out[rows, :] = (x if scale is None else x * scale).astype(bf16)
            return 0

        lax.fori_loop(0, 4, part, 0)

    def save(i, src, dst):
        c = pltpu.make_async_copy(src, dst, sems_out.at[i])
        c.start()
        outs.append(c)

    ins[0].wait()
    ins[1].wait()
    project(hits, w_value, v)
    save(0, v, v_h)

    def turn(i, _):
        vt[i] = transposed(v[block_rows(i), :])
        return 0

    lax.fori_loop(0, HB, turn, 0)
    ins[2].wait()
    project(hits, w_key, k)
    save(1, k, k_h)
    ins[3].wait()
    ins[4].wait()
    project(queries, w_query, q, SCALE)
    save(2, q, q_h)
    ins[5].wait()
    ins[6].wait()

    def grads(i, _):
        x = dot(w_out[...], grad_out[pl.ds(pl.multiple_of(i * 256, 256), 256), :], NT).astype(bf16)
        gatt_t[2 * i] = x[:, :B]
        gatt_t[2 * i + 1] = x[:, B:]
        return 0

    lax.fori_loop(0, 4, grads, 0)

    def query_block(qb, _):
        rows = q[block_rows(qb), :]
        for p in range(PAIRS):
            spread_heads(rows, p, heads_q, masks)
        peak[...] = jnp.full(peak.shape, NEG, f32)
        total[...] = jnp.zeros(total.shape, f32)
        acc[...] = jnp.zeros(acc.shape, f32)

        def body(blocks):
            ps = range(PAIRS)
            scores = [dot(gathered_rows(k, blocks, pair_cols(p)), heads_q[p], NT) for p in ps]
            old = [peak[p] for p in ps]
            new = [jnp.maximum(o, jnp.max(s, axis=0, keepdims=True)) for o, s in zip(old, scores)]
            shrink = [jnp.exp(o - n) for o, n in zip(old, new)]
            expo = [jnp.exp(s - n) for s, n in zip(scores, new)]
            numer = [dot(gathered_cols(vt, blocks, pair_cols(p)), expo[p].astype(bf16)) for p in ps]
            for p in ps:
                peak[p] = new[p]
                total[p] = total[p] * shrink[p] + jnp.sum(expo[p], axis=0, keepdims=True)
                acc[p, :64] = acc[p, :64] * shrink[p][:, :B] + numer[p][:64, :B]
                acc[p, 64:] = acc[p, 64:] * shrink[p][:, B:] + numer[p][64:, B:]

        over_listed(lists, counts, qb, body)
        core, z = qb // 4, lax.rem(qb, 4)
        for p in range(PAIRS):
            some = total[p] > 0.0
            safe = jnp.where(some, total[p], 1.0)
            log_total = jnp.where(some, peak[p] + jnp.log(safe), NEG)
            inverse = 1.0 / safe
            for half, out in enumerate((natt_e.at[core, p, z], natt_o.at[core, z, p])):
                lanes = slice(half * B, (half + 1) * B)
                rows = slice(half * 64, half * 64 + 64)
                part = acc[p, rows] * inverse[:, lanes]
                out[...] = part.astype(bf16)
                grads = gatt_t[qb, p * B + half * 64 : p * B + half * 64 + 64, :].astype(f32)
                h = 2 * p + half
                stats[qb, h : h + 1, :] = log_total[:, lanes]
                stats[qb, 8 + h : 9 + h, :] = jnp.sum(part * grads, axis=0, keepdims=True)
        return 0

    lax.fori_loop(0, QB, query_block, 0)
    for c in outs:
        c.wait()


def place():
    r = lax.axis_index("region")
    return r // 8, lax.rem(r // 2, 4), lax.rem(r, 2)


def index_of(z, y, core):
    return (z * 4 + y) * 2 + core


def remote(src, dst, send, recv, peer):
    return pltpu.make_async_remote_copy(
        src_ref=src, dst_ref=dst, send_sem=send, recv_sem=recv,
        device_id={"region": peer}, device_id_type=MESH,
    )


def greet(peers):
    barrier = pltpu.get_barrier_semaphore()
    for peer in peers:
        pl.semaphore_signal(barrier, inc=1, device_id={"region": peer}, device_id_type=MESH)
    pl.semaphore_wait(barrier, len(peers))


class Links:
    def __init__(self, send, recv):
        self.send, self.recv, self.sent = send, recv, []

    def go(self, src, dst, s, r, peer):
        d = remote(src, dst, self.send.at[s], self.recv.at[r], peer)
        d.start()
        self.sent.append(d)

    def got(self, ref, r, peer):
        remote(ref, ref, self.send.at[r], self.recv.at[r], peer).wait_recv()

    def finish(self):
        for d in self.sent:
            d.wait_send()


def merge(parts):
    peak = parts[0][:, :8]
    for part in parts[1:]:
        peak = jnp.maximum(peak, part[:, :8])
    total = None
    for part in parts:
        w = jnp.exp(part[:, :8] - peak)
        total = w if total is None else total + w
    log_total = peak + jnp.log(total)
    delta = None
    for part in parts:
        d = part[:, 8:] * jnp.exp(part[:, :8] - log_total)
        delta = d if delta is None else delta + d
    return jnp.concatenate([log_total, delta], axis=1)


def softmax_kernel(stats_in, k_h, hits_h, grad_out_h, w_out_h,
                   stats, kt_h, hits_t_h, gatt_h,
                   pair, half_a, half_b, got_a1, got_b1, mid_a, mid_b, got_a2, got_b2,
                   k, hits, grad_out, w_out, kt, hits_t, gatt, send, recv, sems_in, sems_out):
    z, y, core = place()
    sibling = index_of(z, y, 1 - core)
    ys = [lax.rem(y + i, 4) for i in (1, 2, 3)]
    zs = [lax.rem(z + i, 4) for i in (1, 2, 3)]
    y_peers = [index_of(z, v, core) for v in ys]
    z_peers = [index_of(v, y, core) for v in zs]
    ins = loads(((grad_out_h, grad_out), (w_out_h, w_out), (k_h, k), (hits_h, hits)), sems_in)
    greet([sibling] + y_peers + z_peers)
    net = Links(send, recv)
    theirs, mine = pl.ds(4 * (1 - core), 4), 4 * core
    net.go(stats_in.at[theirs], pair, 0, 0, sibling)
    outs = []

    def save(i, src, dst):
        c = pltpu.make_async_copy(src, dst, sems_out.at[i])
        c.start()
        outs.append(c)

    def grad_att(i):
        rows = slice(i * 256, i * 256 + 256)
        gatt[rows, :] = dot(grad_out[rows, :], w_out[...], NT).astype(bf16)

    def turn(src, dst, first, count):
        def one(i, _):
            dst[i] = transposed(src[block_rows(i), :])
            return 0

        lax.fori_loop(first, first + count, one, 0)

    net.got(pair, 0, sibling)
    half_a[...] = merge([stats_in[pl.ds(mine, 2)], pair[:2]])
    half_b[...] = merge([stats_in[pl.ds(mine + 2, 2)], pair[2:]])
    for i in range(3):
        net.go(half_a, got_a1.at[2 - i], 1 + i, 1 + 2 - i, y_peers[i])
        net.go(half_b, got_b1.at[2 - i], 4 + i, 4 + 2 - i, z_peers[i])
    ins[0].wait()
    ins[1].wait()
    grad_att(0)
    grad_att(1)
    for i in range(3):
        net.got(got_a1.at[i], 1 + i, y_peers[i])
        net.got(got_b1.at[i], 4 + i, z_peers[i])
    mid_a[...] = merge([half_a[...], got_a1[0], got_a1[1], got_a1[2]])
    mid_b[...] = merge([half_b[...], got_b1[0], got_b1[1], got_b1[2]])
    for i in range(3):
        net.go(mid_a, got_a2.at[2 - i], 7 + i, 7 + 2 - i, z_peers[i])
        net.go(mid_b, got_b2.at[2 - i], 10 + i, 10 + 2 - i, y_peers[i])
    grad_att(2)
    grad_att(3)
    save(0, gatt, gatt_h)
    for c in ins[2:]:
        c.wait()
    turn(k, kt, 0, 4)
    for i in range(3):
        net.got(got_a2.at[i], 7 + i, z_peers[i])
        net.got(got_b2.at[i], 10 + i, y_peers[i])
    stats[pl.ds(mine, 2)] = merge([mid_a[...], got_a2[0], got_a2[1], got_a2[2]])
    stats[pl.ds(mine + 2, 2)] = merge([mid_b[...], got_b2[0], got_b2[1], got_b2[2]])
    here = stats.at[pl.ds(mine, 4)]
    net.go(here, here, 13, 13, sibling)
    turn(k, kt, 4, 4)
    save(1, kt, kt_h)
    turn(hits, hits_t, 0, 8)
    save(2, hits_t, hits_t_h)
    net.got(stats.at[theirs], 13, sibling)
    net.finish()
    for c in outs:
        c.wait()


def backward_kernel(q, k, v, kt, gatt, stats, stats_own, natt_e, natt_o, hits_t_h, w_key_h, w_value_h, mask_ref,
                    even_out, odd_out, grad_hits,
                    hits_t, w_key, w_value, dk, dv, dkb, dvb, heads_q, heads_g, acc, lists, counts, sems_in):
    ins = loads(((w_key_h, w_key), (w_value_h, w_value), (hits_t_h, hits_t)), sems_in)
    list_blocks(mask_ref, lists, counts)
    masks = lane_masks()
    dk[...] = jnp.zeros(dk.shape, f32)
    dv[...] = jnp.zeros(dv.shape, f32)

    def query_block(qb, _):
        core, z = qb // 4, lax.rem(qb, 4)
        rows, grads = q[block_rows(qb), :], gatt[block_rows(qb), :]
        for p in range(PAIRS):
            spread_heads(rows, p, heads_q, masks)
            spread_heads(grads, p, heads_g, masks)
        acc[...] = jnp.zeros(acc.shape, f32)

        def stat_row(p, base):
            h = base + 2 * p
            return jnp.concatenate([stats[qb, h : h + 1, :], stats[qb, h + 1 : h + 2, :]], axis=1)

        def body(blocks):
            ps = range(PAIRS)
            keys = [gathered_rows(k, blocks, pair_cols(p)) for p in ps]
            vals = [gathered_rows(v, blocks, pair_cols(p)) for p in ps]
            scores = [dot(keys[p], heads_q[p], NT) for p in ps]
            dps = [dot(vals[p], heads_g[p], NT) for p in ps]
            probs = [jnp.exp(scores[p] - stat_row(p, 0)) for p in ps]
            ds = [(probs[p] * (dps[p] - stat_row(p, 8))).astype(bf16) for p in ps]
            dvs = [dot(probs[p].astype(bf16), heads_g[p]) for p in ps]
            dks = [dot(ds[p], heads_q[p]) for p in ps]
            dqs = [dot(gathered_cols(kt, blocks, pair_cols(p)), ds[p]) for p in ps]
            for p in ps:
                for j, b in enumerate(blocks):
                    part = slice(j * B, (j + 1) * B)
                    dv[block_rows(b), pair_cols(p)] += dvs[p][part]
                    dk[block_rows(b), pair_cols(p)] += dks[p][part]
                acc[p, :64] = acc[p, :64] + dqs[p][:64, :B]
                acc[p, 64:] = acc[p, 64:] + dqs[p][64:, B:]

        over_listed(lists, counts, qb, body)
        for p in range(PAIRS):
            for half, (out, natt) in enumerate(
                ((even_out.at[:, core, p, z], natt_e.at[core, p, z]), (odd_out.at[:, core, z, p], natt_o.at[core, z, p]))
            ):
                h = 2 * p + half
                weight = jnp.exp(stats_own[qb, h : h + 1, :] - stats[qb, h : h + 1, :])
                out[0, :64] = (natt[...].astype(f32) * weight).astype(bf16)
                out[1, :64] = (acc[p, half * 64 : half * 64 + 64] * SCALE).astype(bf16)
        return 0

    lax.fori_loop(0, QB, query_block, 0)
    ins[0].wait()
    ins[1].wait()

    def finish(i, _):
        rows = pl.ds(pl.multiple_of(i * 256, 256), 256)
        a, b = dk[rows, :].astype(bf16), dv[rows, :].astype(bf16)
        dkb[rows, :] = a
        dvb[rows, :] = b
        grad_hits[rows, :] = (dot(a, w_key[...], NT) + dot(b, w_value[...], NT)).astype(bf16)
        return 0

    lax.fori_loop(0, 4, finish, 0)
    ins[2].wait()
    for which, grad in enumerate((dkb, dvb)):
        for z in range(4):
            rows = jnp.concatenate([hits_t[i, z * B : (z + 1) * B, :] for i in range(HB)], axis=1)
            part = dot(rows, grad[...]).astype(bf16)
            for p in range(PAIRS):
                for chunk in range(2):
                    lo = 32 * chunk
                    even_out[chunk, which, p, z, 64:] = part[lo : lo + 32, pair_cols(p)]
                    odd_out[chunk, which, z, p, 64:] = part[64 + lo : 96 + lo, pair_cols(p)]


HALVES = (slice(0, 48), slice(48, 96))
FLOWS = 42


def total_kernel(even_in, odd_in, gath_a, gath_b,
                 pair_e, pair_o, half_e, half_o, relay_e, relay_o, near_e, near_o,
                 quarter_e, quarter_o, second_e, second_o, send, recv):
    z, y, core = place()
    sibling = index_of(z, y, 1 - core)
    ys = [lax.rem(y + i, 4) for i in (1, 2, 3)]
    zs = [lax.rem(z + i, 4) for i in (1, 2, 3)]
    y_peers = [index_of(z, v, core) for v in ys]
    z_peers = [index_of(v, y, core) for v in zs]
    greet([sibling] + y_peers + z_peers)
    net = Links(send, recv)
    go, got = net.go, lambda ref, r: net.got(ref, r, sibling)
    along_y, along_z = (y, ys, y_peers), (z, zs, z_peers)

    for c in range(2):
        go(even_in.at[c, 1 - core], pair_e.at[c], c * FLOWS, c * FLOWS, sibling)
        go(odd_in.at[c, 1 - core], pair_o.at[c], c * FLOWS + 1, c * FLOWS + 1, sibling)

    def flows(c):
        b = c * FLOWS
        return (
            (even_in.at[c], pair_e.at[c], half_e.at[c], relay_e.at[c], near_e.at[c], quarter_e.at[c], second_e.at[c],
             along_y, along_z, b, b + 2, b + 14),
            (odd_in.at[c], pair_o.at[c], half_o.at[c], relay_o.at[c], near_o.at[c], quarter_o.at[c], second_o.at[c],
             along_z, along_y, b + 1, b + 8, b + 17),
        )

    for c in range(2):
        for src, pair, half, relay, near, _, _, (_, others, peers), _, s0, s1, _ in flows(c):
            plus, opposite, minus = others
            got(pair, s0)

            def add(j, _):
                half[j] = (src[core, j].astype(f32) + pair[j].astype(f32)).astype(bf16)
                return 0

            lax.fori_loop(0, 4, add, 0)
            first, last = HALVES
            go(half.at[opposite, :, first], relay.at[0], s1, s1, peers[0])
            go(half.at[opposite, :, last], relay.at[1], s1 + 1, s1 + 1, peers[2])
            go(half.at[plus, :, last], near.at[0], s1 + 2, s1 + 2, peers[0])
            go(half.at[minus, :, first], near.at[1], s1 + 3, s1 + 3, peers[2])
    for c in range(2):
        for _, _, half, relay, near, _, _, (_, others, peers), _, _, s1, _ in flows(c):
            plus, opposite, minus = others
            for j, (to, rows, peer) in enumerate(((plus, HALVES[0], peers[0]), (minus, HALVES[1], peers[2]))):
                got(relay.at[j], s1 + j)
                half[to, :, rows] = (half[to, :, rows].astype(f32) + relay[j].astype(f32)).astype(bf16)
                go(half.at[to, :, rows], near.at[2 + j], s1 + 4 + j, s1 + 4 + j, peer)
    for c in range(2):
        for _, _, half, _, near, quarter, second, (own, _, _), (_, others, peers), _, s1, s2 in flows(c):
            for i in (2, 3, 4, 5):
                got(near.at[i - 2], s1 + i)
            for rows, i, j in ((HALVES[0], 1, 2), (HALVES[1], 0, 3)):
                quarter[:, rows] = (
                    half[own, :, rows].astype(f32) + near[i].astype(f32) + near[j].astype(f32)
                ).astype(bf16)
            for i in range(3):
                go(quarter.at[others[i]], second.at[2 - i], s2 + i, s2 + 2 - i, peers[i])
    a1, b1, a2, b2, sa, sb = 20, 23, 26, 30, 34, 38
    for c in range(2):
        base = c * FLOWS
        sums = []
        for _, _, _, _, _, quarter, second, _, (own, _, _), _, _, s2 in flows(c):
            for i in range(3):
                got(second.at[i], s2 + i)
            total = quarter[own].astype(f32)
            for i in range(3):
                total = total + second[i].astype(f32)
            sums.append(total)
        turned = jnp.concatenate([sums[0][:64], sums[1][:64]], axis=0).T
        for half, gath in enumerate((gath_a.at[c, core, z, y], gath_b.at[c, core, y, z])):
            gath[:64] = turned[half * 64 : half * 64 + 64].astype(bf16)
            gath[64:] = sums[half][64:].astype(bf16)
        for i in range(3):
            block = gath_a.at[c, core, z, y]
            go(block, block, base + a1 + i, base + a1 + 2 - i, y_peers[i])
            block = gath_b.at[c, core, y, z]
            go(block, block, base + b1 + i, base + b1 + 2 - i, z_peers[i])

    def gathers(c):
        base = c * FLOWS
        return (
            (gath_a.at[c], z, zs, z_peers, base + a2, base + sa, base + a1, ys),
            (gath_b.at[c], y, ys, y_peers, base + b2, base + sb, base + b1, zs),
        )

    for c in range(2):
        for gath, own, others, peers, s, f, before, fast in gathers(c):
            for i in range(3):
                got(gath.at[core, own, fast[i]], before + i)
            row = gath.at[core, own]
            go(row, row, s, s, peers[0])
            go(row, row, s + 1, s + 1, peers[2])
            go(row, row, f, f, sibling)
    for c in range(2):
        for gath, own, others, peers, s, f, before, fast in gathers(c):
            plus, opposite, minus = others
            got(gath.at[core, minus], s)
            part = gath.at[core, minus, :, HALVES[0]]
            go(part, part, s + 2, s + 2, peers[0])
            got(gath.at[core, plus], s + 1)
            part = gath.at[core, plus, :, HALVES[1]]
            go(part, part, s + 3, s + 3, peers[2])
            row = gath.at[core, minus]
            go(row, row, f + 1, f + 1, sibling)
            row = gath.at[core, plus]
            go(row, row, f + 2, f + 2, sibling)
    for c in range(2):
        for gath, own, others, peers, s, f, before, fast in gathers(c):
            plus, opposite, minus = others
            got(gath.at[core, opposite, :, HALVES[0]], s + 2)
            got(gath.at[core, opposite, :, HALVES[1]], s + 3)
            row = gath.at[core, opposite]
            go(row, row, f + 3, f + 3, sibling)
    for c in range(2):
        for gath, own, others, peers, s, f, before, fast in gathers(c):
            plus, opposite, minus = others
            for i, at in enumerate((own, minus, plus, opposite)):
                got(gath.at[1 - core, at], f + i)
    net.finish()


def final_kernel(queries, grad_out, w_query, w_out, gath_a, gath_b,
                 layer_out, grad_queries, grad_wq, grad_wk, grad_wv, grad_wo,
                 grad_q, attended):
    for qb in range(QB):
        core, z = qb // 4, qb % 4
        for p in range(PAIRS):
            for half in range(2):
                block = gath_a.at[:, core, z, p] if half == 0 else gath_b.at[:, core, p, z]
                rows = slice(qb * B + half * 64, qb * B + half * 64 + 64)
                attended[rows, pair_cols(p)] = block[0, :64]
                grad_q[rows, pair_cols(p)] = block[1, :64]
                out = grad_wk if core == 0 else grad_wv
                local = z * B + half * 64
                out[local : local + 32, pair_cols(p)] = block[0, 64:].astype(f32)
                out[local + 32 : local + 64, pair_cols(p)] = block[1, 64:].astype(f32)

    def rows_block(i, _):
        rows = block_rows(i)
        layer_out[rows, :] = (queries[rows, :].astype(f32) + dot(attended[rows, :], w_out[...])).astype(bf16)
        grad_queries[rows, :] = (grad_out[rows, :].astype(f32) + dot(grad_q[rows, :], w_query[...], NT)).astype(bf16)
        return 0

    lax.fori_loop(0, 8, rows_block, 0)
    for j in range(4):
        cols = pair_cols(j)
        grad_wq[cols, :] = dot(queries[:, cols], grad_q[...], TN)
        grad_wo[cols, :] = dot(attended[:, cols], grad_out[...], TN)


def shaped(*shape, dtype=f32):
    return jax.ShapeDtypeStruct(shape, dtype)


VMEM = pl.BlockSpec(memory_space=pltpu.VMEM)
ANY = pl.BlockSpec(memory_space=pl.ANY)
DMA = pltpu.SemaphoreType.DMA


def scratch(*shape, dtype=bf16):
    return pltpu.VMEM(shape, dtype)


def call(kernel, args, outs, scratch_shapes, collective=None, any_in=(), any_out=()):
    params = {"vmem_limit_bytes": VMEM_LIMIT}
    if collective is not None:
        params |= {"collective_id": collective, "has_side_effects": True}
    return pl.pallas_call(
        kernel,
        out_shape=outs,
        in_specs=[ANY if i in any_in else VMEM for i in range(len(args))],
        out_specs=tuple(ANY if i in any_out else VMEM for i in range(len(outs))),
        scratch_shapes=scratch_shapes,
        compiler_params=pltpu.CompilerParams(**params),
        name=kernel.__name__,
    )(*args)


def on_device(queries_in, hits_in, w_query, w_key, w_value, w_out, mask_list, grad_out):
    full, weight = scratch(N, D), scratch(D, D)
    turned = scratch(HB, D, B)
    spread = scratch(PAIRS, 2 * B, B)
    lists = [pltpu.SMEM((QB, HB + 1), jnp.int32), pltpu.SMEM((QB,), jnp.int32)]
    q, k, v, natt_e, natt_o, stats_own = call(
        forward_kernel,
        (queries_in, hits_in, w_query, w_key, w_value, grad_out, w_out, mask_list),
        (
            shaped(N, D, dtype=bf16), shaped(N, D, dtype=bf16), shaped(N, D, dtype=bf16),
            shaped(2, 4, 4, 64, B, dtype=bf16), shaped(2, 4, 4, 64, B, dtype=bf16), shaped(QB, 16, B),
        ),
        [
            full, full, weight, weight, weight, full, weight, full, full, full,
            turned, turned, spread, scratch(PAIRS, B, B, dtype=f32),
            scratch(PAIRS, 1, 2 * B, dtype=f32), scratch(PAIRS, 1, 2 * B, dtype=f32),
        ] + lists + [DMA((7,)), DMA((3,))],
        any_in=range(7),
        any_out=range(3),
    )
    two = scratch(2, 16, B, dtype=f32)
    three = scratch(3, 2, 16, B, dtype=f32)
    stats, kt, hits_t, gatt = call(
        softmax_kernel,
        (stats_own, k, hits_in, grad_out, w_out),
        (
            shaped(QB, 16, B), shaped(HB, D, B, dtype=bf16), shaped(HB, D, B, dtype=bf16),
            shaped(N, D, dtype=bf16),
        ),
        [
            scratch(4, 16, B, dtype=f32), two, two, three, three, two, two, three, three,
            full, full, full, weight, turned, turned, full, DMA((14,)), DMA((14,)), DMA((4,)), DMA((3,)),
        ],
        collective=0,
        any_in=(1, 2, 3, 4),
        any_out=(1, 2, 3),
    )
    even, odd, grad_hits = call(
        backward_kernel,
        (q, k, v, kt, gatt, stats, stats_own, natt_e, natt_o, hits_t, w_key, w_value, mask_list),
        (shaped(2, 2, 4, 4, 96, B, dtype=bf16), shaped(2, 2, 4, 4, 96, B, dtype=bf16), shaped(N, D, dtype=bf16)),
        [
            turned, weight, weight, scratch(N, D, dtype=f32), scratch(N, D, dtype=f32), full, full,
            spread, spread, scratch(PAIRS, B, B, dtype=f32),
        ] + lists + [DMA((3,))],
        any_in=(9, 10, 11),
    )
    stages = []
    for lead in ((2, 4, 4, 96), (2, 4, 4, 96), (2, 2, 4, 48), (2, 4, 4, 48), (2, 4, 96), (2, 3, 96)):
        stages += [scratch(*lead, B)] * 2
    gath_a, gath_b = call(
        total_kernel,
        (even, odd),
        (shaped(2, 2, 4, 4, 96, B, dtype=bf16), shaped(2, 2, 4, 4, 96, B, dtype=bf16)),
        stages + [DMA((2 * FLOWS,)), DMA((2 * FLOWS,))],
        collective=1,
    )
    layer_out, grad_queries, grad_wq, grad_wk, grad_wv, grad_wo = call(
        final_kernel,
        (queries_in, grad_out, w_query, w_out, gath_a, gath_b),
        (
            shaped(N, D, dtype=bf16), shaped(N, D, dtype=bf16),
            shaped(D, D), shaped(D, D), shaped(D, D), shaped(D, D),
        ),
        [full, full],
    )
    return (layer_out, grad_queries, grad_hits, grad_wq, grad_wk, grad_wv, grad_wo)


def solution(mesh):
    per_event = P("event", None)
    per_region = P(("event", "region"), None)
    return jax.shard_map(
        on_device,
        mesh=mesh,
        in_specs=(per_event, per_region, P(), P(), P(), P(), per_event, per_event),
        out_specs=(per_event, per_event, per_region, per_event, per_event, per_event, per_event),
        check_vma=False,
    )
```

```python
import jax
import jax.numpy as jnp
from jax import lax
from jax.experimental import pallas as pl
from jax.experimental.pallas import tpu as pltpu
from jax.sharding import PartitionSpec as P

f32 = jnp.float32
bf16 = jnp.bfloat16
HEADS = 8
PAIRS = 4
B = 128
QB = 8
HB = 8
D = 512
N = 1024
SCALE = 0.125
NEG = -1e30
MIB = 1024 * 1024
VMEM_LIMIT = 28 * MIB
FORWARD_LIMIT = 53 * MIB
MESH = pl.DeviceIdType.MESH
NN = (((1,), (0,)), ((), ()))
NT = (((1,), (1,)), ((), ()))
TN = (((0,), (0,)), ((), ()))


def dot(a, b, dims=NN):
    return lax.dot_general(a, b, dims, preferred_element_type=f32)


def transposed(block):
    return block.astype(f32).T.astype(block.dtype)


def pair_cols(p):
    return slice(p * B, (p + 1) * B)


def block_rows(i):
    return pl.ds(pl.multiple_of(i * B, B), B)


def list_blocks(mask_ref, lists, counts):
    first = lax.axis_index("region") * HB
    slot = mask_ref[...] - first
    inside = (slot >= 0) & (slot < HB)
    weight = jnp.where(inside, jnp.left_shift(1, jnp.clip(slot, 0, HB - 1)), 0).astype(f32)
    for qb in range(QB):
        bits = jnp.sum(weight[qb : qb + 1, :]).astype(jnp.int32)
        count = jnp.int32(0)
        for hb in range(HB):
            lists[qb, count] = hb
            count = count + (jnp.right_shift(bits, hb) & 1)
        counts[qb] = count


def over_listed(lists, counts, qb, body):
    count = counts[qb]

    def two(i, _):
        body([lists[qb, 2 * i], lists[qb, 2 * i + 1]])
        return 0

    lax.fori_loop(0, count // 2, two, 0)

    @pl.when(lax.rem(count, 2) == 1)
    def _():
        body([lists[qb, count - 1]])


def gathered_rows(ref, blocks, cols):
    return jnp.concatenate([ref[block_rows(b), cols] for b in blocks], axis=0)


def gathered_cols(ref, blocks, rows):
    return jnp.concatenate([ref[b, rows, :] for b in blocks], axis=1)


def lane_masks():
    lane = lax.broadcasted_iota(jnp.int32, (1, B), 1)
    even = jnp.where(lane < 64, 1.0, 0.0)
    return even.astype(bf16), (1.0 - even).astype(bf16)


def spread_heads(rows, p, out, masks):
    block = rows[:, pair_cols(p)]
    out[p, :B] = block * masks[0]
    out[p, B:] = block * masks[1]


def loads(pairs, sems):
    copies = [pltpu.make_async_copy(src, dst, sems.at[i]) for i, (src, dst) in enumerate(pairs)]
    for c in copies:
        c.start()
    return copies


def forward_kernel(queries_h, hits_h, w_query_h, w_key_h, w_value_h, grad_out_h, w_out_h, mask_ref,
                   q_h, k_h, v_h, natt_e, natt_o, stats,
                   queries, hits, w_query, w_key, w_value, grad_out, w_out, q, k, v,
                   gatt_t, heads_q, acc, peak, total, lists, counts, sems_in, sems_out):
    ins = loads(
        ((hits_h, hits), (w_value_h, w_value), (w_key_h, w_key), (queries_h, queries),
         (w_query_h, w_query), (grad_out_h, grad_out), (w_out_h, w_out)), sems_in)
    list_blocks(mask_ref, lists, counts)
    masks = lane_masks()

    def project(src, weight, out, scale=None):
        def part(i, _):
            rows = pl.ds(pl.multiple_of(i * 256, 256), 256)
            x = dot(src[rows, :], weight[...])
            out[rows, :] = (x if scale is None else x * scale).astype(bf16)
            return 0

        lax.fori_loop(0, 4, part, 0)

    ins[0].wait()
    ins[1].wait()
    project(hits, w_value, v)
    saves = loads(((v, v_h),), sems_out)

    ins[2].wait()
    project(hits, w_key, k)
    saves += loads(((k, k_h),), sems_out.at[pl.ds(1, 1)])
    ins[3].wait()
    ins[4].wait()
    project(queries, w_query, q, SCALE)
    saves += loads(((q, q_h),), sems_out.at[pl.ds(2, 1)])
    ins[5].wait()
    ins[6].wait()

    def grads(i, _):
        x = dot(w_out[...], grad_out[pl.ds(pl.multiple_of(i * 256, 256), 256), :], NT).astype(bf16)
        gatt_t[2 * i] = x[:, :B]
        gatt_t[2 * i + 1] = x[:, B:]
        return 0

    lax.fori_loop(0, 4, grads, 0)

    def query_block(qb, _):
        rows = q[block_rows(qb), :]
        for p in range(PAIRS):
            spread_heads(rows, p, heads_q, masks)
        peak[...] = jnp.full(peak.shape, NEG, f32)
        total[...] = jnp.zeros(total.shape, f32)
        acc[...] = jnp.zeros(acc.shape, f32)

        def body(blocks):
            ps = range(PAIRS)
            scores = [dot(gathered_rows(k, blocks, pair_cols(p)), heads_q[p], NT) for p in ps]
            old = [peak[p] for p in ps]
            new = [jnp.maximum(o, jnp.max(s, axis=0, keepdims=True)) for o, s in zip(old, scores)]
            shrink = [jnp.exp(o - n) for o, n in zip(old, new)]
            expo = [jnp.exp(s - n) for s, n in zip(scores, new)]
            numer = [dot(gathered_rows(v, blocks, pair_cols(p)), expo[p].astype(bf16), TN) for p in ps]
            for p in ps:
                peak[p] = new[p]
                total[p] = total[p] * shrink[p] + jnp.sum(expo[p], axis=0, keepdims=True)
                acc[p, :64] = acc[p, :64] * shrink[p][:, :B] + numer[p][:64, :B]
                acc[p, 64:] = acc[p, 64:] * shrink[p][:, B:] + numer[p][64:, B:]

        over_listed(lists, counts, qb, body)
        core, z = qb // 4, lax.rem(qb, 4)
        for p in range(PAIRS):
            some = total[p] > 0.0
            safe = jnp.where(some, total[p], 1.0)
            log_total = jnp.where(some, peak[p] + jnp.log(safe), NEG)
            inverse = 1.0 / safe
            for half, out in enumerate((natt_e.at[core, p, z], natt_o.at[core, z, p])):
                lanes = slice(half * B, (half + 1) * B)
                rows = slice(half * 64, half * 64 + 64)
                part = acc[p, rows] * inverse[:, lanes]
                out[...] = part.astype(bf16)
                grads = gatt_t[qb, p * B + half * 64 : p * B + half * 64 + 64, :].astype(f32)
                h = 2 * p + half
                stats[qb, h : h + 1, :] = log_total[:, lanes]
                stats[qb, 8 + h : 9 + h, :] = jnp.sum(part * grads, axis=0, keepdims=True)
        return 0

    lax.fori_loop(0, QB, query_block, 0)
    for c in saves:
        c.wait()


def place():
    r = lax.axis_index("region")
    return r // 8, lax.rem(r // 2, 4), lax.rem(r, 2)


def index_of(z, y, core):
    return (z * 4 + y) * 2 + core


def remote(src, dst, send, recv, peer):
    return pltpu.make_async_remote_copy(
        src_ref=src, dst_ref=dst, send_sem=send, recv_sem=recv,
        device_id={"region": peer}, device_id_type=MESH,
    )


def greet(peers):
    barrier = pltpu.get_barrier_semaphore()
    for peer in peers:
        pl.semaphore_signal(barrier, inc=1, device_id={"region": peer}, device_id_type=MESH)
    pl.semaphore_wait(barrier, len(peers))


class Links:
    def __init__(self, send, recv):
        self.send, self.recv, self.sent = send, recv, []

    def go(self, src, dst, s, r, peer):
        d = remote(src, dst, self.send.at[s], self.recv.at[r], peer)
        d.start()
        self.sent.append(d)

    def got(self, ref, r, peer):
        remote(ref, ref, self.send.at[r], self.recv.at[r], peer).wait_recv()

    def finish(self):
        for d in self.sent:
            d.wait_send()


def merge(parts):
    peak = parts[0][:, :8]
    for part in parts[1:]:
        peak = jnp.maximum(peak, part[:, :8])
    total = None
    for part in parts:
        w = jnp.exp(part[:, :8] - peak)
        total = w if total is None else total + w
    log_total = peak + jnp.log(total)
    delta = None
    for part in parts:
        d = part[:, 8:] * jnp.exp(part[:, :8] - log_total)
        delta = d if delta is None else delta + d
    return jnp.concatenate([log_total, delta], axis=1)


def softmax_kernel(stats_in, hits, grad_out, w_out,
                   stats, hits_t, gatt,
                   pair, half_a, half_b, got_a1, got_b1, mid_a, mid_b, got_a2, got_b2,
                   send, recv):
    z, y, core = place()
    sibling = index_of(z, y, 1 - core)
    ys = [lax.rem(y + i, 4) for i in (1, 2, 3)]
    zs = [lax.rem(z + i, 4) for i in (1, 2, 3)]
    y_peers = [index_of(z, v, core) for v in ys]
    z_peers = [index_of(v, y, core) for v in zs]
    greet([sibling] + y_peers + z_peers)
    net = Links(send, recv)
    theirs, mine = pl.ds(4 * (1 - core), 4), 4 * core
    net.go(stats_in.at[theirs], pair, 0, 0, sibling)
    def grad_att(i):
        rows = slice(i * 256, i * 256 + 256)
        gatt[rows, :] = dot(grad_out[rows, :], w_out[...], NT).astype(bf16)

    def turn(src, dst, first, count):
        def one(i, _):
            dst[i] = transposed(src[block_rows(i), :])
            return 0

        lax.fori_loop(first, first + count, one, 0)

    net.got(pair, 0, sibling)
    half_a[...] = merge([stats_in[pl.ds(mine, 2)], pair[:2]])
    half_b[...] = merge([stats_in[pl.ds(mine + 2, 2)], pair[2:]])
    for i in range(3):
        net.go(half_a, got_a1.at[2 - i], 1 + i, 1 + 2 - i, y_peers[i])
        net.go(half_b, got_b1.at[2 - i], 4 + i, 4 + 2 - i, z_peers[i])
    grad_att(0)
    grad_att(1)
    for i in range(3):
        net.got(got_a1.at[i], 1 + i, y_peers[i])
        net.got(got_b1.at[i], 4 + i, z_peers[i])
    mid_a[...] = merge([half_a[...], got_a1[0], got_a1[1], got_a1[2]])
    mid_b[...] = merge([half_b[...], got_b1[0], got_b1[1], got_b1[2]])
    for i in range(3):
        net.go(mid_a, got_a2.at[2 - i], 7 + i, 7 + 2 - i, z_peers[i])
        net.go(mid_b, got_b2.at[2 - i], 10 + i, 10 + 2 - i, y_peers[i])
    grad_att(2)
    grad_att(3)
    turn(hits, hits_t, 0, 4)
    for i in range(3):
        net.got(got_a2.at[i], 7 + i, z_peers[i])
        net.got(got_b2.at[i], 10 + i, y_peers[i])
    stats[pl.ds(mine, 2)] = merge([mid_a[...], got_a2[0], got_a2[1], got_a2[2]])
    stats[pl.ds(mine + 2, 2)] = merge([mid_b[...], got_b2[0], got_b2[1], got_b2[2]])
    here = stats.at[pl.ds(mine, 4)]
    net.go(here, here, 13, 13, sibling)
    turn(hits, hits_t, 4, 4)
    net.got(stats.at[theirs], 13, sibling)
    net.finish()


def backward_kernel(q, k, v, gatt, stats, stats_own, natt_e, natt_o, mask_ref,
                    even_out, odd_out, dkb, dvb,
                    dk, dv, heads_q, heads_g, acc, lists, counts):
    list_blocks(mask_ref, lists, counts)
    masks = lane_masks()
    dk[...] = jnp.zeros(dk.shape, f32)
    dv[...] = jnp.zeros(dv.shape, f32)

    def query_block(qb, _):
        core, z = qb // 4, lax.rem(qb, 4)
        rows, grads = q[block_rows(qb), :], gatt[block_rows(qb), :]
        for p in range(PAIRS):
            spread_heads(rows, p, heads_q, masks)
            spread_heads(grads, p, heads_g, masks)
        acc[...] = jnp.zeros(acc.shape, f32)

        def stat_row(p, base):
            h = base + 2 * p
            return jnp.concatenate([stats[qb, h : h + 1, :], stats[qb, h + 1 : h + 2, :]], axis=1)

        def body(blocks):
            ps = range(PAIRS)
            keys = [gathered_rows(k, blocks, pair_cols(p)) for p in ps]
            vals = [gathered_rows(v, blocks, pair_cols(p)) for p in ps]
            scores = [dot(keys[p], heads_q[p], NT) for p in ps]
            dps = [dot(vals[p], heads_g[p], NT) for p in ps]
            probs = [jnp.exp(scores[p] - stat_row(p, 0)) for p in ps]
            ds = [(probs[p] * (dps[p] - stat_row(p, 8))).astype(bf16) for p in ps]
            dvs = [dot(probs[p].astype(bf16), heads_g[p]) for p in ps]
            dks = [dot(ds[p], heads_q[p]) for p in ps]
            dqs = [dot(keys[p], ds[p], TN) for p in ps]
            for p in ps:
                for j, b in enumerate(blocks):
                    part = slice(j * B, (j + 1) * B)
                    dv[block_rows(b), pair_cols(p)] += dvs[p][part]
                    dk[block_rows(b), pair_cols(p)] += dks[p][part]
                acc[p, :64] = acc[p, :64] + dqs[p][:64, :B]
                acc[p, 64:] = acc[p, 64:] + dqs[p][64:, B:]

        over_listed(lists, counts, qb, body)
        for p in range(PAIRS):
            for half, (out, natt) in enumerate(
                ((even_out.at[:, core, p, z], natt_e.at[core, p, z]), (odd_out.at[:, core, z, p], natt_o.at[core, z, p]))
            ):
                h = 2 * p + half
                weight = jnp.exp(stats_own[qb, h : h + 1, :] - stats[qb, h : h + 1, :])
                out[0] = (natt[...].astype(f32) * weight).astype(bf16)
                out[1] = (acc[p, half * 64 : half * 64 + 64] * SCALE).astype(bf16)
        return 0

    lax.fori_loop(0, QB, query_block, 0)
    dkb[...] = dk[...].astype(bf16)
    dvb[...] = dv[...].astype(bf16)


CHUNKS = 3
FLOWS = 34
FAR_FIRST = (1, 0, 2)


def total_kernel(even_in, odd_in, dkb, dvb, hits_t, w_key, w_value, queries, grad_out, w_out,
                 gath_a, gath_b, grad_hits, layer_out, grad_wo,
                 attended, weight_e, weight_o, pair_e, pair_o, half_e, half_o, first_e, first_o, quarter_e, quarter_o, second_e, second_o,
                 send, recv):
    z, y, core = place()
    sibling = index_of(z, y, 1 - core)
    ys = [lax.rem(y + i, 4) for i in (1, 2, 3)]
    zs = [lax.rem(z + i, 4) for i in (1, 2, 3)]
    y_peers = [index_of(z, v, core) for v in ys]
    z_peers = [index_of(v, y, core) for v in zs]
    greet([sibling] + y_peers + z_peers)
    net = Links(send, recv)
    go, got = net.go, lambda ref, r: net.got(ref, r, sibling)
    along_y, along_z = (y, ys, y_peers), (z, zs, z_peers)

    sources = [(even_in.at[c], odd_in.at[c]) for c in range(2)] + [(weight_e, weight_o)]

    def send_pair(c):
        for i, (src, pair) in enumerate(zip(sources[c], (pair_e, pair_o))):
            go(src.at[1 - core], pair.at[c], c * FLOWS + i, c * FLOWS + i, sibling)

    def weight_grads(c):
        left = jnp.concatenate([hits_t[i] for i in range(HB)], axis=1)
        for which, grad in enumerate((dkb, dvb)):
            for side in range(2):
                part = dot(left, grad[:, side * 256 : side * 256 + 256]).astype(bf16)
                for p in (2 * side, 2 * side + 1):
                    for v in range(4):
                        tile = part[v * B : (v + 1) * B, pair_cols(p - 2 * side)]
                        weight_e[which, p, v] = tile[:64]
                        weight_o[which, v, p] = tile[64:]
        send_pair(c)

    def hit_grads(half):
        for i in range(2 * half, 2 * half + 2):
            rows = slice(i * 256, i * 256 + 256)
            x = dot(dkb[rows, :], w_key[...], NT) + dot(dvb[rows, :], w_value[...], NT)
            grad_hits[rows, :] = x.astype(bf16)

    def attended_products(c):
        for qb in range(QB):
            for p in range(PAIRS):
                parts = gath_a[c, qb // 4, qb % 4, p], gath_b[c, qb // 4, p, qb % 4]
                for half, block in enumerate(parts):
                    row = qb * B + half * 64
                    attended[row : row + 64, pair_cols(p)] = block
        for i in range(4):
            rows = slice(i * 256, i * 256 + 256)
            layer_out[rows, :] = (queries[rows, :].astype(f32) + dot(attended[rows, :], w_out[...])).astype(bf16)
        for i in range(2):
            cols = slice(i * 256, i * 256 + 256)
            grad_wo[cols, :] = dot(attended[:, cols], grad_out[...], TN)

    def flows(c):
        b = c * FLOWS
        return (
            (sources[c][0].at[core], pair_e.at[c], half_e.at[c], first_e.at[c], quarter_e.at[c], second_e.at[c],
             along_y, along_z, b, b + 2, b + 8),
            (sources[c][1].at[core], pair_o.at[c], half_o.at[c], first_o.at[c], quarter_o.at[c], second_o.at[c],
             along_z, along_y, b + 1, b + 5, b + 11),
        )

    def add_cores(c):
        for src, pair, half, first, _, _, (_, others, peers), _, s0, s1, _ in flows(c):
            got(pair, s0)
            for i in FAR_FIRST:
                half[i] = src[others[i]] + pair[others[i]]
                go(half.at[i], first.at[2 - i], s1 + i, s1 + 2 - i, peers[i])

    def add_first(c):
        for src, pair, _, first, quarter, second, (own, _, _), (_, others, peers), _, s1, s2 in flows(c):
            total = src[own].astype(f32) + pair[own].astype(f32)
            for i in range(3):
                got(first.at[i], s1 + i)
                total = total + first[i].astype(f32)
            quarter[...] = total.astype(bf16)
            for i in FAR_FIRST:
                go(quarter.at[others[i]], second.at[2 - i], s2 + i, s2 + 2 - i, peers[i])

    a1, b1, a2, b2, sa, sb = 14, 17, 20, 23, 26, 30

    def add_second(c):
        base = c * FLOWS
        sums = []
        for _, _, _, _, quarter, second, _, (own, _, _), _, _, s2 in flows(c):
            total = quarter[own].astype(f32)
            for i in range(3):
                got(second.at[i], s2 + i)
                total = total + second[i].astype(f32)
            sums.append(total)
        if c < 2:
            turned = jnp.concatenate(sums, axis=0).T
            sums = [turned[:64], turned[64:]]
        blocks = gath_a.at[c, core, z, y], gath_b.at[c, core, y, z]
        for block, part in zip(blocks, sums):
            block[...] = part.astype(bf16)
        for i in FAR_FIRST:
            go(blocks[0], blocks[0], base + a1 + i, base + a1 + 2 - i, y_peers[i])
            go(blocks[1], blocks[1], base + b1 + i, base + b1 + 2 - i, z_peers[i])

    def gathers(c):
        base = c * FLOWS
        return (
            (gath_a.at[c], z, zs, z_peers, base + a2, base + sa, base + a1, ys),
            (gath_b.at[c], y, ys, y_peers, base + b2, base + sb, base + b1, zs),
        )

    def pass_row(c):
        for gath, own, others, peers, s, f, before, fast in gathers(c):
            for i in range(3):
                got(gath.at[core, own, fast[i]], before + i)
            row = gath.at[core, own]
            for i in FAR_FIRST:
                go(row, row, s + i, s + 2 - i, peers[i])
            go(row, row, f + 3, f + 3, sibling)

    def pass_sibling(c):
        for gath, own, others, peers, s, f, before, fast in gathers(c):
            for i in (0, 2, 1):
                row = gath.at[core, others[i]]
                got(row, s + i)
                go(row, row, f + i, f + i, sibling)

    def from_sibling(c):
        for gath, own, others, peers, s, f, before, fast in gathers(c):
            for i in range(3):
                got(gath.at[1 - core, others[i]], f + i)
            got(gath.at[1 - core, own], f + 3)

    for step, c in (
        (send_pair, 0), (send_pair, 1), (add_cores, 0), (add_cores, 1), (weight_grads, 2), (add_first, 0),
        (add_first, 1), (add_cores, 2), (hit_grads, 0), (add_second, 0), (add_second, 1), (hit_grads, 1),
        (add_first, 2), (pass_row, 0), (pass_row, 1), (add_second, 2), (pass_sibling, 0), (pass_sibling, 1),
        (pass_row, 2), (from_sibling, 0), (attended_products, 0), (pass_sibling, 2), (from_sibling, 1),
        (from_sibling, 2),
    ):
        step(c)
    net.finish()


def final_kernel(queries, grad_out, w_query, gath_a, gath_b, grad_hits_in, layer_in, grad_wo_in, *refs):
    outs, bufs = refs[:7], refs[7:11]
    grad_q, sems = refs[11:]
    grad_queries, grad_wq, grad_wk, grad_wv = bufs
    ready = (layer_in, grad_queries, grad_hits_in, grad_wq, grad_wk, grad_wv, grad_wo_in)
    saves = []

    def save(i):
        c = pltpu.make_async_copy(ready[i], outs[i], sems.at[i])
        c.start()
        saves.append(c)

    for i in (0, 2, 6):
        save(i)

    def blocks(chunk, qb, p):
        core, z = qb // 4, qb % 4
        return gath_a[chunk, core, z, p], gath_b[chunk, core, p, z]

    def place_blocks(chunk, qb, p, out, row):
        for half, block in enumerate(blocks(chunk, qb, p)):
            out[row + half * 64 : row + half * 64 + 64, pair_cols(p)] = block.astype(out.dtype)

    for qb in range(QB):
        for p in range(PAIRS):
            place_blocks(2, qb, p, grad_wk if qb < 4 else grad_wv, (qb % 4) * B)
            place_blocks(1, qb, p, grad_q, qb * B)
        if qb == 3:
            save(4)
    save(5)

    for j in range(2):
        cols = slice(j * 256, j * 256 + 256)
        grad_wq[cols, :] = dot(queries[:, cols], grad_q[...], TN)
    save(3)
    for i in range(4):
        rows = slice(i * 256, i * 256 + 256)
        grad_queries[rows, :] = (grad_out[rows, :].astype(f32) + dot(grad_q[rows, :], w_query[...], NT)).astype(bf16)
    save(1)
    for c in saves:
        c.wait()


def shaped(*shape, dtype=f32):
    return jax.ShapeDtypeStruct(shape, dtype)


VMEM = pl.BlockSpec(memory_space=pltpu.VMEM)
ANY = pl.BlockSpec(memory_space=pl.ANY)
DMA = pltpu.SemaphoreType.DMA


def scratch(*shape, dtype=bf16):
    return pltpu.VMEM(shape, dtype)


def call(kernel, args, outs, scratch_shapes, collective=None, any_in=(), any_out=(), vmem=VMEM_LIMIT):
    params = {"vmem_limit_bytes": vmem}
    if collective is not None:
        params |= {"collective_id": collective, "has_side_effects": True}
    return pl.pallas_call(
        kernel,
        out_shape=outs,
        in_specs=[ANY if i in any_in else VMEM for i in range(len(args))],
        out_specs=tuple(ANY if i in any_out else VMEM for i in range(len(outs))),
        scratch_shapes=scratch_shapes,
        compiler_params=pltpu.CompilerParams(**params),
        name=kernel.__name__,
    )(*args)


STAGE_SHAPES = ((3, 4, 4, 64), (3, 3, 4, 64), (3, 3, 4, 64), (3, 4, 64), (3, 3, 64))


def on_device(queries_in, hits_in, w_query, w_key, w_value, w_out, mask_list, grad_out):
    full, weight = scratch(N, D), scratch(D, D)
    turned = scratch(HB, D, B)
    spread = scratch(PAIRS, 2 * B, B)
    lists = [pltpu.SMEM((QB, HB + 1), jnp.int32), pltpu.SMEM((QB,), jnp.int32)]
    q, k, v, natt_e, natt_o, stats_own = call(
        forward_kernel,
        (queries_in, hits_in, w_query, w_key, w_value, grad_out, w_out, mask_list),
        (
            shaped(N, D, dtype=bf16), shaped(N, D, dtype=bf16), shaped(N, D, dtype=bf16),
            shaped(2, 4, 4, 64, B, dtype=bf16), shaped(2, 4, 4, 64, B, dtype=bf16), shaped(QB, 16, B),
        ),
        [
            full, full, weight, weight, weight, full, weight, full, full, full,
            turned, spread, scratch(PAIRS, B, B, dtype=f32),
            scratch(PAIRS, 1, 2 * B, dtype=f32), scratch(PAIRS, 1, 2 * B, dtype=f32),
        ] + lists + [DMA((7,)), DMA((3,))],
        any_in=range(7),
        any_out=range(3),
        vmem=FORWARD_LIMIT,
    )
    two = scratch(2, 16, B, dtype=f32)
    three = scratch(3, 2, 16, B, dtype=f32)
    stats, hits_t, gatt = call(
        softmax_kernel,
        (stats_own, hits_in, grad_out, w_out),
        (
            shaped(QB, 16, B), shaped(HB, D, B, dtype=bf16),
            shaped(N, D, dtype=bf16),
        ),
        [
            scratch(4, 16, B, dtype=f32), two, two, three, three, two, two, three, three,
            DMA((14,)), DMA((14,)),
        ],
        collective=0,
        vmem=8 * MIB,
    )
    even, odd, dkb, dvb = call(
        backward_kernel,
        (q, k, v, gatt, stats, stats_own, natt_e, natt_o, mask_list),
        (
            shaped(2, 2, 4, 4, 64, B, dtype=bf16), shaped(2, 2, 4, 4, 64, B, dtype=bf16),
            shaped(N, D, dtype=bf16), shaped(N, D, dtype=bf16),
        ),
        [
            scratch(N, D, dtype=f32), scratch(N, D, dtype=f32),
            spread, spread, scratch(PAIRS, B, B, dtype=f32),
        ] + lists,
        vmem=20 * MIB,
    )
    stages = [full, scratch(2, 4, 4, 64, B), scratch(2, 4, 4, 64, B)]
    for lead in STAGE_SHAPES:
        stages += [scratch(*lead, B)] * 2
    gath_a, gath_b, grad_hits, layer_out, grad_wo = call(
        total_kernel,
        (even, odd, dkb, dvb, hits_t, w_key, w_value, queries_in, grad_out, w_out),
        (
            shaped(3, 2, 4, 4, 64, B, dtype=bf16), shaped(3, 2, 4, 4, 64, B, dtype=bf16),
            shaped(N, D, dtype=bf16), shaped(N, D, dtype=bf16), shaped(D, D),
        ),
        stages + [DMA((CHUNKS * FLOWS,)), DMA((CHUNKS * FLOWS,))],
        collective=1,
        vmem=20 * MIB,
    )
    square = scratch(D, D, dtype=f32)
    layer_out, grad_queries, grad_hits, grad_wq, grad_wk, grad_wv, grad_wo = call(
        final_kernel,
        (queries_in, grad_out, w_query, gath_a, gath_b, grad_hits, layer_out, grad_wo),
        (
            shaped(N, D, dtype=bf16), shaped(N, D, dtype=bf16), shaped(N, D, dtype=bf16),
            shaped(D, D), shaped(D, D), shaped(D, D), shaped(D, D),
        ),
        [full, square, square, square, full, DMA((7,))],
        any_in=(5, 6, 7),
        any_out=range(7),
        vmem=14 * MIB,
    )
    return (layer_out, grad_queries, grad_hits, grad_wq, grad_wk, grad_wv, grad_wo)


def solution(mesh):
    per_event = P("event", None)
    per_region = P(("event", "region"), None)
    return jax.shard_map(
        on_device,
        mesh=mesh,
        in_specs=(per_event, per_region, P(), P(), P(), P(), per_event, per_event),
        out_specs=(per_event, per_event, per_region, per_event, per_event, per_event, per_event),
        check_vma=False,
    )
```

```python
import jax
import jax.numpy as jnp
from jax import lax
from jax.experimental import pallas as pl
from jax.experimental.pallas import tpu as pltpu
from jax.sharding import PartitionSpec as P

f32 = jnp.float32
bf16 = jnp.bfloat16
HEADS = 8
PAIRS = 4
B = 128
QB = 8
HB = 8
D = 512
N = 1024
SCALE = 0.125
NEG = -1e30
MIB = 1024 * 1024
VMEM_LIMIT = 28 * MIB
FORWARD_LIMIT = 53 * MIB
MESH = pl.DeviceIdType.MESH
NN = (((1,), (0,)), ((), ()))
NT = (((1,), (1,)), ((), ()))
TN = (((0,), (0,)), ((), ()))


def dot(a, b, dims=NN):
    return lax.dot_general(a, b, dims, preferred_element_type=f32)


def transposed(block):
    return block.astype(f32).T.astype(block.dtype)


def pair_cols(p):
    return slice(p * B, (p + 1) * B)


def block_rows(i):
    return pl.ds(pl.multiple_of(i * B, B), B)


def list_blocks(mask_ref, lists, counts):
    first = lax.axis_index("region") * HB
    slot = mask_ref[...] - first
    inside = (slot >= 0) & (slot < HB)
    weight = jnp.where(inside, jnp.left_shift(1, jnp.clip(slot, 0, HB - 1)), 0).astype(f32)
    for qb in range(QB):
        bits = jnp.sum(weight[qb : qb + 1, :]).astype(jnp.int32)
        count = jnp.int32(0)
        for hb in range(HB):
            lists[qb, count] = hb
            count = count + (jnp.right_shift(bits, hb) & 1)
        counts[qb] = count


def list_pairs(mask_ref, pairs):
    first = lax.axis_index("region") * HB
    slot = mask_ref[...] - first
    inside = (slot >= 0) & (slot < HB)
    weight = jnp.where(inside, jnp.left_shift(1, jnp.clip(slot, 0, HB - 1)), 0).astype(f32)
    count = jnp.int32(0)
    for qb in range(QB):
        bits = jnp.sum(weight[qb : qb + 1, :]).astype(jnp.int32)
        for hb in range(HB):
            pairs[0, count] = qb
            pairs[1, count] = hb
            count = count + (jnp.right_shift(bits, hb) & 1)
    for i in range(2):
        pairs[0, count + i] = QB
        pairs[1, count + i] = 0
    return count


def over_listed(lists, counts, qb, body):
    count = counts[qb]

    def two(i, _):
        body([lists[qb, 2 * i], lists[qb, 2 * i + 1]])
        return 0

    lax.fori_loop(0, count // 2, two, 0)

    @pl.when(lax.rem(count, 2) == 1)
    def _():
        body([lists[qb, count - 1]])


def gathered_rows(ref, blocks, cols):
    return jnp.concatenate([ref[block_rows(b), cols] for b in blocks], axis=0)


def gathered_cols(ref, blocks, rows):
    return jnp.concatenate([ref[b, rows, :] for b in blocks], axis=1)


def lane_masks():
    lane = lax.broadcasted_iota(jnp.int32, (1, B), 1)
    even = jnp.where(lane < 64, 1.0, 0.0)
    return even.astype(bf16), (1.0 - even).astype(bf16)


def spread_heads(rows, p, out, masks):
    block = rows[:, pair_cols(p)]
    out[p, :B] = block * masks[0]
    out[p, B:] = block * masks[1]


def loads(pairs, sems):
    copies = [pltpu.make_async_copy(src, dst, sems.at[i]) for i, (src, dst) in enumerate(pairs)]
    for c in copies:
        c.start()
    return copies


def forward_kernel(queries_h, hits_h, w_query_h, w_key_h, w_value_h, grad_out_h, w_out_h, mask_ref,
                   q_h, k_h, v_h, natt_e, natt_o, stats,
                   queries, hits, w_query, w_key, w_value, grad_out, w_out, q, k, v,
                   gatt_t, heads_q, acc, peak, total, scores_a, scores_b, pairs, sems_in, sems_out):
    ins = loads(
        ((hits_h, hits), (w_value_h, w_value), (w_key_h, w_key), (queries_h, queries),
         (w_query_h, w_query), (grad_out_h, grad_out), (w_out_h, w_out)), sems_in)
    masks = lane_masks()

    def project(src, weight, out, scale=None):
        for i in range(2):
            rows = slice(i * 512, i * 512 + 512)
            x = dot(src[rows, :], weight[...])
            out[rows, :] = (x if scale is None else x * scale).astype(bf16)

    ins[0].wait()
    ins[1].wait()
    project(hits, w_value, v)
    saves = loads(((v, v_h),), sems_out)

    ins[2].wait()
    project(hits, w_key, k)
    saves += loads(((k, k_h),), sems_out.at[pl.ds(1, 1)])
    ins[3].wait()
    ins[4].wait()
    project(queries, w_query, q, SCALE)
    saves += loads(((q, q_h),), sems_out.at[pl.ds(2, 1)])
    count = list_pairs(mask_ref, pairs)
    ins[5].wait()
    ins[6].wait()

    for i in range(4):
        x = dot(w_out[...], grad_out[i * 256 : i * 256 + 256, :], NT).astype(bf16)
        gatt_t[2 * i] = x[:, :B]
        gatt_t[2 * i + 1] = x[:, B:]

    def spread(qb, _):
        rows = q[block_rows(qb), :]
        for p in range(PAIRS):
            spread_heads(rows, p, heads_q.at[qb], masks)
        return 0

    lax.fori_loop(0, QB, spread, 0)
    heads_q[QB] = jnp.zeros(heads_q.shape[1:], bf16)
    peak[...] = jnp.full(peak.shape, NEG, f32)
    total[...] = jnp.zeros(total.shape, f32)
    acc[...] = jnp.zeros(acc.shape, f32)
    ps = range(PAIRS)

    def score(i, out):
        qb, hb = pairs[0, i], pairs[1, i]
        for p in ps:
            out[p] = dot(k[block_rows(hb), pair_cols(p)], heads_q[qb, p], NT)

    def add(i, scores):
        qb, hb = pairs[0, i], pairs[1, i]
        old = [peak[qb, p] for p in ps]
        new = [jnp.maximum(old[p], jnp.max(scores[p], axis=0, keepdims=True)) for p in ps]
        shrink = [jnp.exp(old[p] - new[p]) for p in ps]
        expo = [jnp.exp(scores[p] - new[p]) for p in ps]
        numer = [dot(v[block_rows(hb), pair_cols(p)], expo[p].astype(bf16), TN) for p in ps]
        for p in ps:
            peak[qb, p] = new[p]
            total[qb, p] = total[qb, p] * shrink[p] + jnp.sum(expo[p], axis=0, keepdims=True)
            acc[qb, p, :64] = acc[qb, p, :64] * shrink[p][:, :B] + numer[p][:64, :B]
            acc[qb, p, 64:] = acc[qb, p, 64:] * shrink[p][:, B:] + numer[p][64:, B:]

    score(0, scores_a)

    def two(j, _):
        score(2 * j + 1, scores_b)
        add(2 * j, scores_a)
        score(2 * j + 2, scores_a)
        add(2 * j + 1, scores_b)
        return 0

    lax.fori_loop(0, (count + 1) // 2, two, 0)

    def query_block(qb, _):
        core, z = qb // 4, lax.rem(qb, 4)
        for p in range(PAIRS):
            some = total[qb, p] > 0.0
            safe = jnp.where(some, total[qb, p], 1.0)
            log_total = jnp.where(some, peak[qb, p] + jnp.log(safe), NEG)
            inverse = 1.0 / safe
            for half, out in enumerate((natt_e.at[core, p, z], natt_o.at[core, z, p])):
                lanes = slice(half * B, (half + 1) * B)
                rows = slice(half * 64, half * 64 + 64)
                part = acc[qb, p, rows] * inverse[:, lanes]
                out[...] = part.astype(bf16)
                grads = gatt_t[qb, p * B + half * 64 : p * B + half * 64 + 64, :].astype(f32)
                h = 2 * p + half
                stats[qb, h : h + 1, :] = log_total[:, lanes]
                stats[qb, 8 + h : 9 + h, :] = jnp.sum(part * grads, axis=0, keepdims=True)
        return 0

    lax.fori_loop(0, QB, query_block, 0)
    for c in saves:
        c.wait()


def place():
    r = lax.axis_index("region")
    return r // 8, lax.rem(r // 2, 4), lax.rem(r, 2)


def index_of(z, y, core):
    return (z * 4 + y) * 2 + core


def remote(src, dst, send, recv, peer):
    return pltpu.make_async_remote_copy(
        src_ref=src, dst_ref=dst, send_sem=send, recv_sem=recv,
        device_id={"region": peer}, device_id_type=MESH,
    )


def greet(peers):
    barrier = pltpu.get_barrier_semaphore()
    for peer in peers:
        pl.semaphore_signal(barrier, inc=1, device_id={"region": peer}, device_id_type=MESH)
    pl.semaphore_wait(barrier, len(peers))


class Links:
    def __init__(self, send, recv):
        self.send, self.recv, self.sent = send, recv, []

    def go(self, src, dst, s, r, peer):
        d = remote(src, dst, self.send.at[s], self.recv.at[r], peer)
        d.start()
        self.sent.append(d)

    def got(self, ref, r, peer):
        remote(ref, ref, self.send.at[r], self.recv.at[r], peer).wait_recv()

    def finish(self):
        for d in self.sent:
            d.wait_send()


def merge(parts):
    peak = parts[0][:, :8]
    for part in parts[1:]:
        peak = jnp.maximum(peak, part[:, :8])
    total = None
    for part in parts:
        w = jnp.exp(part[:, :8] - peak)
        total = w if total is None else total + w
    log_total = peak + jnp.log(total)
    delta = None
    for part in parts:
        d = part[:, 8:] * jnp.exp(part[:, :8] - log_total)
        delta = d if delta is None else delta + d
    return jnp.concatenate([log_total, delta], axis=1)


def softmax_kernel(stats_in, hits, grad_out, w_out,
                   stats, hits_t, gatt,
                   pair, half_a, half_b, got_a1, got_b1, mid_a, mid_b, got_a2, got_b2,
                   send, recv):
    z, y, core = place()
    sibling = index_of(z, y, 1 - core)
    ys = [lax.rem(y + i, 4) for i in (1, 2, 3)]
    zs = [lax.rem(z + i, 4) for i in (1, 2, 3)]
    y_peers = [index_of(z, v, core) for v in ys]
    z_peers = [index_of(v, y, core) for v in zs]
    greet([sibling] + y_peers + z_peers)
    net = Links(send, recv)
    theirs, mine = pl.ds(4 * (1 - core), 4), 4 * core
    net.go(stats_in.at[theirs], pair, 0, 0, sibling)
    def grad_att(i):
        rows = slice(i * 256, i * 256 + 256)
        gatt[rows, :] = dot(grad_out[rows, :], w_out[...], NT).astype(bf16)

    def turn(src, dst, first, count):
        def one(i, _):
            dst[i] = transposed(src[block_rows(i), :])
            return 0

        lax.fori_loop(first, first + count, one, 0)

    net.got(pair, 0, sibling)
    half_a[...] = merge([stats_in[pl.ds(mine, 2)], pair[:2]])
    half_b[...] = merge([stats_in[pl.ds(mine + 2, 2)], pair[2:]])
    for i in range(3):
        net.go(half_a, got_a1.at[2 - i], 1 + i, 1 + 2 - i, y_peers[i])
        net.go(half_b, got_b1.at[2 - i], 4 + i, 4 + 2 - i, z_peers[i])
    grad_att(0)
    grad_att(1)
    for i in range(3):
        net.got(got_a1.at[i], 1 + i, y_peers[i])
        net.got(got_b1.at[i], 4 + i, z_peers[i])
    mid_a[...] = merge([half_a[...], got_a1[0], got_a1[1], got_a1[2]])
    mid_b[...] = merge([half_b[...], got_b1[0], got_b1[1], got_b1[2]])
    for i in range(3):
        net.go(mid_a, got_a2.at[2 - i], 7 + i, 7 + 2 - i, z_peers[i])
        net.go(mid_b, got_b2.at[2 - i], 10 + i, 10 + 2 - i, y_peers[i])
    grad_att(2)
    grad_att(3)
    turn(hits, hits_t, 0, 4)
    for i in range(3):
        net.got(got_a2.at[i], 7 + i, z_peers[i])
        net.got(got_b2.at[i], 10 + i, y_peers[i])
    stats[pl.ds(mine, 2)] = merge([mid_a[...], got_a2[0], got_a2[1], got_a2[2]])
    stats[pl.ds(mine + 2, 2)] = merge([mid_b[...], got_b2[0], got_b2[1], got_b2[2]])
    here = stats.at[pl.ds(mine, 4)]
    net.go(here, here, 13, 13, sibling)
    turn(hits, hits_t, 4, 4)
    net.got(stats.at[theirs], 13, sibling)
    net.finish()


def backward_kernel(q, k, v, gatt, stats, stats_own, natt_e, natt_o, mask_ref,
                    even_out, odd_out, dkb, dvb,
                    dk, dv, heads_q, heads_g, acc, lists, counts):
    list_blocks(mask_ref, lists, counts)
    masks = lane_masks()
    dk[...] = jnp.zeros(dk.shape, f32)
    dv[...] = jnp.zeros(dv.shape, f32)

    def query_block(qb, _):
        core, z = qb // 4, lax.rem(qb, 4)
        rows, grads = q[block_rows(qb), :], gatt[block_rows(qb), :]
        for p in range(PAIRS):
            spread_heads(rows, p, heads_q, masks)
            spread_heads(grads, p, heads_g, masks)
        acc[...] = jnp.zeros(acc.shape, f32)

        def stat_row(p, base):
            h = base + 2 * p
            return jnp.concatenate([stats[qb, h : h + 1, :], stats[qb, h + 1 : h + 2, :]], axis=1)

        def body(blocks):
            ps = range(PAIRS)
            keys = [gathered_rows(k, blocks, pair_cols(p)) for p in ps]
            vals = [gathered_rows(v, blocks, pair_cols(p)) for p in ps]
            scores = [dot(keys[p], heads_q[p], NT) for p in ps]
            dps = [dot(vals[p], heads_g[p], NT) for p in ps]
            probs = [jnp.exp(scores[p] - stat_row(p, 0)) for p in ps]
            ds = [(probs[p] * (dps[p] - stat_row(p, 8))).astype(bf16) for p in ps]
            dvs = [dot(probs[p].astype(bf16), heads_g[p]) for p in ps]
            dks = [dot(ds[p], heads_q[p]) for p in ps]
            dqs = [dot(keys[p], ds[p], TN) for p in ps]
            for p in ps:
                for j, b in enumerate(blocks):
                    part = slice(j * B, (j + 1) * B)
                    dv[block_rows(b), pair_cols(p)] += dvs[p][part]
                    dk[block_rows(b), pair_cols(p)] += dks[p][part]
                acc[p, :64] = acc[p, :64] + dqs[p][:64, :B]
                acc[p, 64:] = acc[p, 64:] + dqs[p][64:, B:]

        over_listed(lists, counts, qb, body)
        for p in range(PAIRS):
            for half, (out, natt) in enumerate(
                ((even_out.at[:, core, p, z], natt_e.at[core, p, z]), (odd_out.at[:, core, z, p], natt_o.at[core, z, p]))
            ):
                h = 2 * p + half
                weight = jnp.exp(stats_own[qb, h : h + 1, :] - stats[qb, h : h + 1, :])
                out[0] = (natt[...].astype(f32) * weight).astype(bf16)
                out[1] = (acc[p, half * 64 : half * 64 + 64] * SCALE).astype(bf16)
        return 0

    lax.fori_loop(0, QB, query_block, 0)
    dkb[...] = dk[...].astype(bf16)
    dvb[...] = dv[...].astype(bf16)


CHUNKS = 3
FLOWS = 34
FAR_FIRST = (1, 0, 2)


def total_kernel(even_in, odd_in, dkb, dvb, hits_t, w_key, w_value, queries, grad_out, w_out,
                 gath_a, gath_b, grad_hits, layer_out, grad_wo,
                 attended, weight_e, weight_o, pair_e, pair_o, half_e, half_o, first_e, first_o, quarter_e, quarter_o, second_e, second_o,
                 send, recv):
    z, y, core = place()
    sibling = index_of(z, y, 1 - core)
    ys = [lax.rem(y + i, 4) for i in (1, 2, 3)]
    zs = [lax.rem(z + i, 4) for i in (1, 2, 3)]
    y_peers = [index_of(z, v, core) for v in ys]
    z_peers = [index_of(v, y, core) for v in zs]
    greet([sibling] + y_peers + z_peers)
    net = Links(send, recv)
    go, got = net.go, lambda ref, r: net.got(ref, r, sibling)
    along_y, along_z = (y, ys, y_peers), (z, zs, z_peers)

    sources = [(even_in.at[c], odd_in.at[c]) for c in range(2)] + [(weight_e, weight_o)]

    def send_pair(c):
        for i, (src, pair) in enumerate(zip(sources[c], (pair_e, pair_o))):
            go(src.at[1 - core], pair.at[c], c * FLOWS + i, c * FLOWS + i, sibling)

    def weight_grads(c):
        left = jnp.concatenate([hits_t[i] for i in range(HB)], axis=1)
        for which, grad in enumerate((dkb, dvb)):
            for side in range(2):
                part = dot(left, grad[:, side * 256 : side * 256 + 256]).astype(bf16)
                for p in (2 * side, 2 * side + 1):
                    for v in range(4):
                        tile = part[v * B : (v + 1) * B, pair_cols(p - 2 * side)]
                        weight_e[which, p, v] = tile[:64]
                        weight_o[which, v, p] = tile[64:]
        send_pair(c)

    def hit_grads(half):
        for i in range(2 * half, 2 * half + 2):
            rows = slice(i * 256, i * 256 + 256)
            x = dot(dkb[rows, :], w_key[...], NT) + dot(dvb[rows, :], w_value[...], NT)
            grad_hits[rows, :] = x.astype(bf16)

    def attended_products(c):
        for qb in range(QB):
            for p in range(PAIRS):
                parts = gath_a[c, qb // 4, qb % 4, p], gath_b[c, qb // 4, p, qb % 4]
                for half, block in enumerate(parts):
                    row = qb * B + half * 64
                    attended[row : row + 64, pair_cols(p)] = block
        for i in range(4):
            rows = slice(i * 256, i * 256 + 256)
            layer_out[rows, :] = (queries[rows, :].astype(f32) + dot(attended[rows, :], w_out[...])).astype(bf16)
        for i in range(2):
            cols = slice(i * 256, i * 256 + 256)
            grad_wo[cols, :] = dot(attended[:, cols], grad_out[...], TN)

    def flows(c):
        b = c * FLOWS
        return (
            (sources[c][0].at[core], pair_e.at[c], half_e.at[c], first_e.at[c], quarter_e.at[c], second_e.at[c],
             along_y, along_z, b, b + 2, b + 8),
            (sources[c][1].at[core], pair_o.at[c], half_o.at[c], first_o.at[c], quarter_o.at[c], second_o.at[c],
             along_z, along_y, b + 1, b + 5, b + 11),
        )

    def add_cores(c):
        for src, pair, half, first, _, _, (_, others, peers), _, s0, s1, _ in flows(c):
            got(pair, s0)
            for i in FAR_FIRST:
                half[i] = src[others[i]] + pair[others[i]]
                go(half.at[i], first.at[2 - i], s1 + i, s1 + 2 - i, peers[i])

    def add_first(c):
        for src, pair, _, first, quarter, second, (own, _, _), (_, others, peers), _, s1, s2 in flows(c):
            total = src[own].astype(f32) + pair[own].astype(f32)
            for i in range(3):
                got(first.at[i], s1 + i)
                total = total + first[i].astype(f32)
            quarter[...] = total.astype(bf16)
            for i in FAR_FIRST:
                go(quarter.at[others[i]], second.at[2 - i], s2 + i, s2 + 2 - i, peers[i])

    a1, b1, a2, b2, sa, sb = 14, 17, 20, 23, 26, 30

    def add_second(c):
        base = c * FLOWS
        sums = []
        for _, _, _, _, quarter, second, _, (own, _, _), _, _, s2 in flows(c):
            total = quarter[own].astype(f32)
            for i in range(3):
                got(second.at[i], s2 + i)
                total = total + second[i].astype(f32)
            sums.append(total)
        if c < 2:
            turned = jnp.concatenate(sums, axis=0).T
            sums = [turned[:64], turned[64:]]
        blocks = gath_a.at[c, core, z, y], gath_b.at[c, core, y, z]
        for block, part in zip(blocks, sums):
            block[...] = part.astype(bf16)
        for i in FAR_FIRST:
            go(blocks[0], blocks[0], base + a1 + i, base + a1 + 2 - i, y_peers[i])
            go(blocks[1], blocks[1], base + b1 + i, base + b1 + 2 - i, z_peers[i])

    def gathers(c):
        base = c * FLOWS
        return (
            (gath_a.at[c], z, zs, z_peers, base + a2, base + sa, base + a1, ys),
            (gath_b.at[c], y, ys, y_peers, base + b2, base + sb, base + b1, zs),
        )

    def pass_row(c):
        for gath, own, others, peers, s, f, before, fast in gathers(c):
            for i in range(3):
                got(gath.at[core, own, fast[i]], before + i)
            row = gath.at[core, own]
            for i in FAR_FIRST:
                go(row, row, s + i, s + 2 - i, peers[i])
            go(row, row, f + 3, f + 3, sibling)

    def pass_sibling(c):
        for gath, own, others, peers, s, f, before, fast in gathers(c):
            for i in (0, 2, 1):
                row = gath.at[core, others[i]]
                got(row, s + i)
                go(row, row, f + i, f + i, sibling)

    def from_sibling(c):
        for gath, own, others, peers, s, f, before, fast in gathers(c):
            for i in range(3):
                got(gath.at[1 - core, others[i]], f + i)
            got(gath.at[1 - core, own], f + 3)

    for step, c in (
        (send_pair, 0), (send_pair, 1), (add_cores, 0), (weight_grads, 2), (add_cores, 1), (add_first, 0),
        (add_cores, 2), (add_first, 1), (hit_grads, 0), (add_second, 0), (add_first, 2), (add_second, 1),
        (hit_grads, 1), (pass_row, 0), (add_second, 2), (pass_row, 1), (pass_sibling, 0), (pass_row, 2),
        (pass_sibling, 1), (from_sibling, 0), (attended_products, 0), (pass_sibling, 2), (from_sibling, 1),
        (from_sibling, 2),
    ):
        step(c)
    net.finish()


def final_kernel(queries, grad_out, w_query, gath_a, gath_b, grad_hits_in, layer_in, grad_wo_in, *refs):
    outs, bufs = refs[:7], refs[7:11]
    grad_q, sems = refs[11:]
    grad_queries, grad_wq, grad_wk, grad_wv = bufs
    ready = (layer_in, grad_queries, grad_hits_in, grad_wq, grad_wk, grad_wv, grad_wo_in)
    saves = []

    def save(i):
        c = pltpu.make_async_copy(ready[i], outs[i], sems.at[i])
        c.start()
        saves.append(c)

    for i in (0, 2, 6):
        save(i)

    def blocks(chunk, qb, p):
        core, z = qb // 4, qb % 4
        return gath_a[chunk, core, z, p], gath_b[chunk, core, p, z]

    def place_blocks(chunk, qb, p, out, row):
        for half, block in enumerate(blocks(chunk, qb, p)):
            out[row + half * 64 : row + half * 64 + 64, pair_cols(p)] = block.astype(out.dtype)

    for qb in range(QB):
        for p in range(PAIRS):
            place_blocks(2, qb, p, grad_wk if qb < 4 else grad_wv, (qb % 4) * B)
            place_blocks(1, qb, p, grad_q, qb * B)
        if qb == 3:
            save(4)
    save(5)

    for j in range(2):
        cols = slice(j * 256, j * 256 + 256)
        grad_wq[cols, :] = dot(queries[:, cols], grad_q[...], TN)
    save(3)
    for i in range(4):
        rows = slice(i * 256, i * 256 + 256)
        grad_queries[rows, :] = (grad_out[rows, :].astype(f32) + dot(grad_q[rows, :], w_query[...], NT)).astype(bf16)
    save(1)
    for c in saves:
        c.wait()


def shaped(*shape, dtype=f32):
    return jax.ShapeDtypeStruct(shape, dtype)


VMEM = pl.BlockSpec(memory_space=pltpu.VMEM)
ANY = pl.BlockSpec(memory_space=pl.ANY)
DMA = pltpu.SemaphoreType.DMA


def scratch(*shape, dtype=bf16):
    return pltpu.VMEM(shape, dtype)


def call(kernel, args, outs, scratch_shapes, collective=None, any_in=(), any_out=(), vmem=VMEM_LIMIT, flops=None):
    params = {"vmem_limit_bytes": vmem}
    if collective is not None:
        params |= {"collective_id": collective, "has_side_effects": True}
    return pl.pallas_call(
        kernel,
        out_shape=outs,
        in_specs=[ANY if i in any_in else VMEM for i in range(len(args))],
        out_specs=tuple(ANY if i in any_out else VMEM for i in range(len(outs))),
        scratch_shapes=scratch_shapes,
        compiler_params=pltpu.CompilerParams(**params),
        cost_estimate=flops and pl.CostEstimate(flops=flops, bytes_accessed=4 * MIB, transcendentals=0),
        name=kernel.__name__,
    )(*args)


STAGE_SHAPES = ((3, 4, 4, 64), (3, 3, 4, 64), (3, 3, 4, 64), (3, 4, 64), (3, 3, 64))


def on_device(queries_in, hits_in, w_query, w_key, w_value, w_out, mask_list, grad_out):
    full, weight = scratch(N, D), scratch(D, D)
    turned = scratch(HB, D, B)
    spread = scratch(PAIRS, 2 * B, B)
    lists = [pltpu.SMEM((QB, HB + 1), jnp.int32), pltpu.SMEM((QB,), jnp.int32)]
    q, k, v, natt_e, natt_o, stats_own = call(
        forward_kernel,
        (queries_in, hits_in, w_query, w_key, w_value, grad_out, w_out, mask_list),
        (
            shaped(N, D, dtype=bf16), shaped(N, D, dtype=bf16), shaped(N, D, dtype=bf16),
            shaped(2, 4, 4, 64, B, dtype=bf16), shaped(2, 4, 4, 64, B, dtype=bf16), shaped(QB, 16, B),
        ),
        [
            full, full, weight, weight, weight, full, weight, full, full, full,
            turned, scratch(QB + 1, PAIRS, 2 * B, B), scratch(QB + 1, PAIRS, B, B, dtype=f32),
            scratch(QB + 1, PAIRS, 1, 2 * B, dtype=f32), scratch(QB + 1, PAIRS, 1, 2 * B, dtype=f32),
            scratch(PAIRS, B, 2 * B, dtype=f32), scratch(PAIRS, B, 2 * B, dtype=f32),
            pltpu.SMEM((2, QB * HB + 2), jnp.int32), DMA((7,)), DMA((3,)),
        ],
        any_in=range(7),
        any_out=range(3),
        vmem=FORWARD_LIMIT,
    )
    two = scratch(2, 16, B, dtype=f32)
    three = scratch(3, 2, 16, B, dtype=f32)
    stats, hits_t, gatt = call(
        softmax_kernel,
        (stats_own, hits_in, grad_out, w_out),
        (
            shaped(QB, 16, B), shaped(HB, D, B, dtype=bf16),
            shaped(N, D, dtype=bf16),
        ),
        [
            scratch(4, 16, B, dtype=f32), two, two, three, three, two, two, three, three,
            DMA((14,)), DMA((14,)),
        ],
        collective=0,
        vmem=8 * MIB,
        flops=2 * 10**10,
    )
    even, odd, dkb, dvb = call(
        backward_kernel,
        (q, k, v, gatt, stats, stats_own, natt_e, natt_o, mask_list),
        (
            shaped(2, 2, 4, 4, 64, B, dtype=bf16), shaped(2, 2, 4, 4, 64, B, dtype=bf16),
            shaped(N, D, dtype=bf16), shaped(N, D, dtype=bf16),
        ),
        [
            scratch(N, D, dtype=f32), scratch(N, D, dtype=f32),
            spread, spread, scratch(PAIRS, B, B, dtype=f32),
        ] + lists,
        vmem=20 * MIB,
    )
    stages = [full, scratch(2, 4, 4, 64, B), scratch(2, 4, 4, 64, B)]
    for lead in STAGE_SHAPES:
        stages += [scratch(*lead, B)] * 2
    gath_a, gath_b, grad_hits, layer_out, grad_wo = call(
        total_kernel,
        (even, odd, dkb, dvb, hits_t, w_key, w_value, queries_in, grad_out, w_out),
        (
            shaped(3, 2, 4, 4, 64, B, dtype=bf16), shaped(3, 2, 4, 4, 64, B, dtype=bf16),
            shaped(N, D, dtype=bf16), shaped(N, D, dtype=bf16), shaped(D, D),
        ),
        stages + [DMA((CHUNKS * FLOWS,)), DMA((CHUNKS * FLOWS,))],
        collective=1,
        vmem=20 * MIB,
    )
    square = scratch(D, D, dtype=f32)
    layer_out, grad_queries, grad_hits, grad_wq, grad_wk, grad_wv, grad_wo = call(
        final_kernel,
        (queries_in, grad_out, w_query, gath_a, gath_b, grad_hits, layer_out, grad_wo),
        (
            shaped(N, D, dtype=bf16), shaped(N, D, dtype=bf16), shaped(N, D, dtype=bf16),
            shaped(D, D), shaped(D, D), shaped(D, D), shaped(D, D),
        ),
        [full, square, square, square, full, DMA((7,))],
        any_in=(5, 6, 7),
        any_out=range(7),
        vmem=14 * MIB,
    )
    return (layer_out, grad_queries, grad_hits, grad_wq, grad_wk, grad_wv, grad_wo)


def solution(mesh):
    per_event = P("event", None)
    per_region = P(("event", "region"), None)
    return jax.shard_map(
        on_device,
        mesh=mesh,
        in_specs=(per_event, per_region, P(), P(), P(), P(), per_event, per_event),
        out_specs=(per_event, per_event, per_region, per_event, per_event, per_event, per_event),
        check_vma=False,
    )
```

```python
import jax
import jax.numpy as jnp
from jax import lax
from jax.experimental import pallas as pl
from jax.experimental.pallas import tpu as pltpu
from jax.sharding import PartitionSpec as P

f32 = jnp.float32
bf16 = jnp.bfloat16
HEADS = 8
PAIRS = 4
B = 128
QB = 8
HB = 8
D = 512
N = 1024
SCALE = 0.125
NEG = -1e30
MIB = 1024 * 1024
VMEM_LIMIT = 28 * MIB
FORWARD_LIMIT = 53 * MIB
MESH = pl.DeviceIdType.MESH
NN = (((1,), (0,)), ((), ()))
NT = (((1,), (1,)), ((), ()))
TN = (((0,), (0,)), ((), ()))


def dot(a, b, dims=NN):
    return lax.dot_general(a, b, dims, preferred_element_type=f32)


def transposed(block):
    return block.astype(f32).T.astype(block.dtype)


def pair_cols(p):
    return slice(p * B, (p + 1) * B)


def block_rows(i):
    return pl.ds(pl.multiple_of(i * B, B), B)


def list_blocks(mask_ref, lists, counts):
    first = lax.axis_index("region") * HB
    slot = mask_ref[...] - first
    inside = (slot >= 0) & (slot < HB)
    weight = jnp.where(inside, jnp.left_shift(1, jnp.clip(slot, 0, HB - 1)), 0).astype(f32)
    for qb in range(QB):
        bits = jnp.sum(weight[qb : qb + 1, :]).astype(jnp.int32)
        count = jnp.int32(0)
        for hb in range(HB):
            lists[qb, count] = hb
            count = count + (jnp.right_shift(bits, hb) & 1)
        counts[qb] = count


def list_pairs(mask_ref, pairs):
    first = lax.axis_index("region") * HB
    slot = mask_ref[...] - first
    inside = (slot >= 0) & (slot < HB)
    weight = jnp.where(inside, jnp.left_shift(1, jnp.clip(slot, 0, HB - 1)), 0).astype(f32)
    count = jnp.int32(0)
    for qb in range(QB):
        bits = jnp.sum(weight[qb : qb + 1, :]).astype(jnp.int32)
        for hb in range(HB):
            pairs[0, count] = qb
            pairs[1, count] = hb
            count = count + (jnp.right_shift(bits, hb) & 1)
    for i in range(2):
        pairs[0, count + i] = QB
        pairs[1, count + i] = 0
    return count


def over_listed(lists, counts, qb, body):
    count = counts[qb]

    def two(i, _):
        body([lists[qb, 2 * i], lists[qb, 2 * i + 1]])
        return 0

    lax.fori_loop(0, count // 2, two, 0)

    @pl.when(lax.rem(count, 2) == 1)
    def _():
        body([lists[qb, count - 1]])


def gathered_rows(ref, blocks, cols):
    return jnp.concatenate([ref[block_rows(b), cols] for b in blocks], axis=0)


def gathered_cols(ref, blocks, rows):
    return jnp.concatenate([ref[b, rows, :] for b in blocks], axis=1)


def lane_masks():
    lane = lax.broadcasted_iota(jnp.int32, (1, B), 1)
    even = jnp.where(lane < 64, 1.0, 0.0)
    return even.astype(bf16), (1.0 - even).astype(bf16)


def spread_heads(rows, p, out, masks):
    block = rows[:, pair_cols(p)]
    out[p, :B] = block * masks[0]
    out[p, B:] = block * masks[1]


def loads(pairs, sems):
    copies = [pltpu.make_async_copy(src, dst, sems.at[i]) for i, (src, dst) in enumerate(pairs)]
    for c in copies:
        c.start()
    return copies


def forward_kernel(queries_h, hits_h, w_query_h, w_key_h, w_value_h, grad_out_h, w_out_h, mask_ref,
                   q_h, k_h, v_h, natt_e, natt_o, stats,
                   queries, hits, w_query, w_key, w_value, grad_out, w_out, q, k, v,
                   gatt_t, heads_q, acc, peak, total, scores_a, scores_b, pairs, sems_in, sems_out):
    ins = loads(
        ((hits_h, hits), (w_value_h, w_value), (w_key_h, w_key), (queries_h, queries),
         (w_query_h, w_query), (grad_out_h, grad_out), (w_out_h, w_out)), sems_in)
    masks = lane_masks()

    def project(src, weight, out, scale=None):
        for i in range(2):
            rows = slice(i * 512, i * 512 + 512)
            x = dot(src[rows, :], weight[...])
            out[rows, :] = (x if scale is None else x * scale).astype(bf16)

    ins[0].wait()
    ins[1].wait()
    project(hits, w_value, v)
    saves = loads(((v, v_h),), sems_out)

    ins[2].wait()
    project(hits, w_key, k)
    saves += loads(((k, k_h),), sems_out.at[pl.ds(1, 1)])
    ins[3].wait()
    ins[4].wait()
    project(queries, w_query, q, SCALE)
    saves += loads(((q, q_h),), sems_out.at[pl.ds(2, 1)])
    count = list_pairs(mask_ref, pairs)
    ins[5].wait()
    ins[6].wait()

    for i in range(4):
        x = dot(w_out[...], grad_out[i * 256 : i * 256 + 256, :], NT).astype(bf16)
        gatt_t[2 * i] = x[:, :B]
        gatt_t[2 * i + 1] = x[:, B:]

    def spread(qb, _):
        rows = q[block_rows(qb), :]
        for p in range(PAIRS):
            spread_heads(rows, p, heads_q.at[qb], masks)
        return 0

    lax.fori_loop(0, QB, spread, 0)
    heads_q[QB] = jnp.zeros(heads_q.shape[1:], bf16)
    peak[...] = jnp.full(peak.shape, NEG, f32)
    total[...] = jnp.zeros(total.shape, f32)
    acc[...] = jnp.zeros(acc.shape, f32)
    ps = range(PAIRS)

    def score(i, out):
        qb, hb = pairs[0, i], pairs[1, i]
        for p in ps:
            out[p] = dot(k[block_rows(hb), pair_cols(p)], heads_q[qb, p], NT)

    def add(i, scores):
        qb, hb = pairs[0, i], pairs[1, i]
        old = [peak[qb, p] for p in ps]
        new = [jnp.maximum(old[p], jnp.max(scores[p], axis=0, keepdims=True)) for p in ps]
        shrink = [jnp.exp(old[p] - new[p]) for p in ps]
        expo = [jnp.exp(scores[p] - new[p]) for p in ps]
        numer = [dot(v[block_rows(hb), pair_cols(p)], expo[p].astype(bf16), TN) for p in ps]
        for p in ps:
            peak[qb, p] = new[p]
            total[qb, p] = total[qb, p] * shrink[p] + jnp.sum(expo[p], axis=0, keepdims=True)
            acc[qb, p, :64] = acc[qb, p, :64] * shrink[p][:, :B] + numer[p][:64, :B]
            acc[qb, p, 64:] = acc[qb, p, 64:] * shrink[p][:, B:] + numer[p][64:, B:]

    score(0, scores_a)

    def two(j, _):
        score(2 * j + 1, scores_b)
        add(2 * j, scores_a)
        score(2 * j + 2, scores_a)
        add(2 * j + 1, scores_b)
        return 0

    lax.fori_loop(0, (count + 1) // 2, two, 0)

    def query_block(qb, _):
        core, z = qb // 4, lax.rem(qb, 4)
        for p in range(PAIRS):
            some = total[qb, p] > 0.0
            safe = jnp.where(some, total[qb, p], 1.0)
            log_total = jnp.where(some, peak[qb, p] + jnp.log(safe), NEG)
            inverse = 1.0 / safe
            for half, out in enumerate((natt_e.at[core, p, z], natt_o.at[core, z, p])):
                lanes = slice(half * B, (half + 1) * B)
                rows = slice(half * 64, half * 64 + 64)
                part = acc[qb, p, rows] * inverse[:, lanes]
                out[...] = part.astype(bf16)
                grads = gatt_t[qb, p * B + half * 64 : p * B + half * 64 + 64, :].astype(f32)
                h = 2 * p + half
                stats[qb, h : h + 1, :] = log_total[:, lanes]
                stats[qb, 8 + h : 9 + h, :] = jnp.sum(part * grads, axis=0, keepdims=True)
        return 0

    lax.fori_loop(0, QB, query_block, 0)
    for c in saves:
        c.wait()


def place():
    r = lax.axis_index("region")
    return r // 8, lax.rem(r // 2, 4), lax.rem(r, 2)


def index_of(z, y, core):
    return (z * 4 + y) * 2 + core


def remote(src, dst, send, recv, peer):
    return pltpu.make_async_remote_copy(
        src_ref=src, dst_ref=dst, send_sem=send, recv_sem=recv,
        device_id={"region": peer}, device_id_type=MESH,
    )


def greet(peers):
    barrier = pltpu.get_barrier_semaphore()
    for peer in peers:
        pl.semaphore_signal(barrier, inc=1, device_id={"region": peer}, device_id_type=MESH)
    pl.semaphore_wait(barrier, len(peers))


class Links:
    def __init__(self, send, recv):
        self.send, self.recv, self.sent = send, recv, []

    def go(self, src, dst, s, r, peer):
        d = remote(src, dst, self.send.at[s], self.recv.at[r], peer)
        d.start()
        self.sent.append(d)

    def got(self, ref, r, peer):
        remote(ref, ref, self.send.at[r], self.recv.at[r], peer).wait_recv()

    def finish(self):
        for d in self.sent:
            d.wait_send()


def merge(parts):
    peak = parts[0][:, :8]
    for part in parts[1:]:
        peak = jnp.maximum(peak, part[:, :8])
    total = None
    for part in parts:
        w = jnp.exp(part[:, :8] - peak)
        total = w if total is None else total + w
    log_total = peak + jnp.log(total)
    delta = None
    for part in parts:
        d = part[:, 8:] * jnp.exp(part[:, :8] - log_total)
        delta = d if delta is None else delta + d
    return jnp.concatenate([log_total, delta], axis=1)


def softmax_kernel(stats_in, hits, grad_out, w_out,
                   stats, hits_t, gatt,
                   pair, half_a, half_b, got_a1, got_b1, mid_a, mid_b, got_a2, got_b2,
                   send, recv):
    z, y, core = place()
    sibling = index_of(z, y, 1 - core)
    ys = [lax.rem(y + i, 4) for i in (1, 2, 3)]
    zs = [lax.rem(z + i, 4) for i in (1, 2, 3)]
    y_peers = [index_of(z, v, core) for v in ys]
    z_peers = [index_of(v, y, core) for v in zs]
    greet([sibling] + y_peers + z_peers)
    net = Links(send, recv)
    theirs, mine = pl.ds(4 * (1 - core), 4), 4 * core
    net.go(stats_in.at[theirs], pair, 0, 0, sibling)
    def grad_att(i):
        rows = slice(i * 256, i * 256 + 256)
        gatt[rows, :] = dot(grad_out[rows, :], w_out[...], NT).astype(bf16)

    def turn(src, dst, first, count):
        def one(i, _):
            dst[i] = transposed(src[block_rows(i), :])
            return 0

        lax.fori_loop(first, first + count, one, 0)

    net.got(pair, 0, sibling)
    half_a[...] = merge([stats_in[pl.ds(mine, 2)], pair[:2]])
    half_b[...] = merge([stats_in[pl.ds(mine + 2, 2)], pair[2:]])
    for i in range(3):
        net.go(half_a, got_a1.at[2 - i], 1 + i, 1 + 2 - i, y_peers[i])
        net.go(half_b, got_b1.at[2 - i], 4 + i, 4 + 2 - i, z_peers[i])
    grad_att(0)
    grad_att(1)
    for i in range(3):
        net.got(got_a1.at[i], 1 + i, y_peers[i])
        net.got(got_b1.at[i], 4 + i, z_peers[i])
    mid_a[...] = merge([half_a[...], got_a1[0], got_a1[1], got_a1[2]])
    mid_b[...] = merge([half_b[...], got_b1[0], got_b1[1], got_b1[2]])
    for i in range(3):
        net.go(mid_a, got_a2.at[2 - i], 7 + i, 7 + 2 - i, z_peers[i])
        net.go(mid_b, got_b2.at[2 - i], 10 + i, 10 + 2 - i, y_peers[i])
    grad_att(2)
    grad_att(3)
    turn(hits, hits_t, 0, 4)
    for i in range(3):
        net.got(got_a2.at[i], 7 + i, z_peers[i])
        net.got(got_b2.at[i], 10 + i, y_peers[i])
    stats[pl.ds(mine, 2)] = merge([mid_a[...], got_a2[0], got_a2[1], got_a2[2]])
    stats[pl.ds(mine + 2, 2)] = merge([mid_b[...], got_b2[0], got_b2[1], got_b2[2]])
    here = stats.at[pl.ds(mine, 4)]
    net.go(here, here, 13, 13, sibling)
    turn(hits, hits_t, 4, 4)
    net.got(stats.at[theirs], 13, sibling)
    net.finish()


def backward_kernel(q, k, v, gatt, stats, stats_own, natt_e, natt_o, mask_ref,
                    even_out, odd_out, dkb, dvb,
                    dk, dv, heads_q, heads_g, acc, lists, counts):
    list_blocks(mask_ref, lists, counts)
    masks = lane_masks()
    dk[...] = jnp.zeros(dk.shape, f32)
    dv[...] = jnp.zeros(dv.shape, f32)

    def query_block(qb, _):
        core, z = qb // 4, lax.rem(qb, 4)
        rows, grads = q[block_rows(qb), :], gatt[block_rows(qb), :]
        for p in range(PAIRS):
            spread_heads(rows, p, heads_q, masks)
            spread_heads(grads, p, heads_g, masks)
        acc[...] = jnp.zeros(acc.shape, f32)

        def stat_row(p, base):
            h = base + 2 * p
            return jnp.concatenate([stats[qb, h : h + 1, :], stats[qb, h + 1 : h + 2, :]], axis=1)

        def some_heads(blocks, ps):
            keys = {p: gathered_rows(k, blocks, pair_cols(p)) for p in ps}
            vals = {p: gathered_rows(v, blocks, pair_cols(p)) for p in ps}
            scores = {p: dot(keys[p], heads_q[p], NT) for p in ps}
            dps = {p: dot(vals[p], heads_g[p], NT) for p in ps}
            probs = {p: jnp.exp(scores[p] - stat_row(p, 0)) for p in ps}
            ds = {p: (probs[p] * (dps[p] - stat_row(p, 8))).astype(bf16) for p in ps}
            dvs = {p: dot(probs[p].astype(bf16), heads_g[p]) for p in ps}
            dks = {p: dot(ds[p], heads_q[p]) for p in ps}
            dqs = {p: dot(keys[p], ds[p], TN) for p in ps}
            for p in ps:
                for j, b in enumerate(blocks):
                    part = slice(j * B, (j + 1) * B)
                    dv[block_rows(b), pair_cols(p)] += dvs[p][part]
                    dk[block_rows(b), pair_cols(p)] += dks[p][part]
                acc[p, :64] = acc[p, :64] + dqs[p][:64, :B]
                acc[p, 64:] = acc[p, 64:] + dqs[p][64:, B:]

        def body(blocks):
            at_once = PAIRS // len(blocks)
            for p in range(0, PAIRS, at_once):
                some_heads(blocks, range(p, p + at_once))

        over_listed(lists, counts, qb, body)
        for p in range(PAIRS):
            for half, (out, natt) in enumerate(
                ((even_out.at[:, core, p, z], natt_e.at[core, p, z]), (odd_out.at[:, core, z, p], natt_o.at[core, z, p]))
            ):
                h = 2 * p + half
                weight = jnp.exp(stats_own[qb, h : h + 1, :] - stats[qb, h : h + 1, :])
                out[0] = (natt[...].astype(f32) * weight).astype(bf16)
                out[1] = (acc[p, half * 64 : half * 64 + 64] * SCALE).astype(bf16)
        return 0

    lax.fori_loop(0, QB, query_block, 0)
    dkb[...] = dk[...].astype(bf16)
    dvb[...] = dv[...].astype(bf16)


CHUNKS = 3
FLOWS = 34
FAR_FIRST = (1, 0, 2)


def total_kernel(even_in, odd_in, dkb, dvb, hits_t, w_key, w_value, queries, grad_out, w_out,
                 gath_a, gath_b, grad_hits, layer_out, grad_wo,
                 attended, weight_e, weight_o, pair_e, pair_o, half_e, half_o, first_e, first_o, quarter_e, quarter_o, second_e, second_o,
                 send, recv):
    z, y, core = place()
    sibling = index_of(z, y, 1 - core)
    ys = [lax.rem(y + i, 4) for i in (1, 2, 3)]
    zs = [lax.rem(z + i, 4) for i in (1, 2, 3)]
    y_peers = [index_of(z, v, core) for v in ys]
    z_peers = [index_of(v, y, core) for v in zs]
    greet([sibling] + y_peers + z_peers)
    net = Links(send, recv)
    go, got = net.go, lambda ref, r: net.got(ref, r, sibling)
    along_y, along_z = (y, ys, y_peers), (z, zs, z_peers)

    sources = [(even_in.at[c], odd_in.at[c]) for c in range(2)] + [(weight_e, weight_o)]

    def send_pair(c):
        for i, (src, pair) in enumerate(zip(sources[c], (pair_e, pair_o))):
            go(src.at[1 - core], pair.at[c], c * FLOWS + i, c * FLOWS + i, sibling)

    def weight_grads(c):
        left = jnp.concatenate([hits_t[i] for i in range(HB)], axis=1)
        for which, grad in enumerate((dkb, dvb)):
            for side in range(2):
                part = dot(left, grad[:, side * 256 : side * 256 + 256]).astype(bf16)
                for p in (2 * side, 2 * side + 1):
                    for v in range(4):
                        tile = part[v * B : (v + 1) * B, pair_cols(p - 2 * side)]
                        weight_e[which, p, v] = tile[:64]
                        weight_o[which, v, p] = tile[64:]
        send_pair(c)

    def hit_grads(half):
        for i in range(2 * half, 2 * half + 2):
            rows = slice(i * 256, i * 256 + 256)
            x = dot(dkb[rows, :], w_key[...], NT) + dot(dvb[rows, :], w_value[...], NT)
            grad_hits[rows, :] = x.astype(bf16)

    def attended_products(c):
        for qb in range(QB):
            for p in range(PAIRS):
                parts = gath_a[c, qb // 4, qb % 4, p], gath_b[c, qb // 4, p, qb % 4]
                for half, block in enumerate(parts):
                    row = qb * B + half * 64
                    attended[row : row + 64, pair_cols(p)] = block
        for i in range(4):
            rows = slice(i * 256, i * 256 + 256)
            layer_out[rows, :] = (queries[rows, :].astype(f32) + dot(attended[rows, :], w_out[...])).astype(bf16)
        for i in range(2):
            cols = slice(i * 256, i * 256 + 256)
            grad_wo[cols, :] = dot(attended[:, cols], grad_out[...], TN)

    def flows(c):
        b = c * FLOWS
        return (
            (sources[c][0].at[core], pair_e.at[c], half_e.at[c], first_e.at[c], quarter_e.at[c], second_e.at[c],
             along_y, along_z, b, b + 2, b + 8),
            (sources[c][1].at[core], pair_o.at[c], half_o.at[c], first_o.at[c], quarter_o.at[c], second_o.at[c],
             along_z, along_y, b + 1, b + 5, b + 11),
        )

    def add_cores(c):
        for src, pair, half, first, _, _, (_, others, peers), _, s0, s1, _ in flows(c):
            got(pair, s0)
            for i in FAR_FIRST:
                half[i] = src[others[i]] + pair[others[i]]
                go(half.at[i], first.at[2 - i], s1 + i, s1 + 2 - i, peers[i])

    def add_first(c):
        for src, pair, _, first, quarter, second, (own, _, _), (_, others, peers), _, s1, s2 in flows(c):
            total = src[own].astype(f32) + pair[own].astype(f32)
            for i in range(3):
                got(first.at[i], s1 + i)
                total = total + first[i].astype(f32)
            quarter[...] = total.astype(bf16)
            for i in FAR_FIRST:
                go(quarter.at[others[i]], second.at[2 - i], s2 + i, s2 + 2 - i, peers[i])

    a1, b1, a2, b2, sa, sb = 14, 17, 20, 23, 26, 30

    def add_second(c):
        base = c * FLOWS
        sums = []
        for _, _, _, _, quarter, second, _, (own, _, _), _, _, s2 in flows(c):
            total = quarter[own].astype(f32)
            for i in range(3):
                got(second.at[i], s2 + i)
                total = total + second[i].astype(f32)
            sums.append(total)
        if c < 2:
            turned = jnp.concatenate(sums, axis=0).T
            sums = [turned[:64], turned[64:]]
        blocks = gath_a.at[c, core, z, y], gath_b.at[c, core, y, z]
        for block, part in zip(blocks, sums):
            block[...] = part.astype(bf16)
        for i in FAR_FIRST:
            go(blocks[0], blocks[0], base + a1 + i, base + a1 + 2 - i, y_peers[i])
            go(blocks[1], blocks[1], base + b1 + i, base + b1 + 2 - i, z_peers[i])

    def gathers(c):
        base = c * FLOWS
        return (
            (gath_a.at[c], z, zs, z_peers, base + a2, base + sa, base + a1, ys),
            (gath_b.at[c], y, ys, y_peers, base + b2, base + sb, base + b1, zs),
        )

    def pass_row(c):
        for gath, own, others, peers, s, f, before, fast in gathers(c):
            for i in range(3):
                got(gath.at[core, own, fast[i]], before + i)
            row = gath.at[core, own]
            for i in FAR_FIRST:
                go(row, row, s + i, s + 2 - i, peers[i])
            go(row, row, f + 3, f + 3, sibling)

    def pass_sibling(c):
        for gath, own, others, peers, s, f, before, fast in gathers(c):
            for i in (0, 2, 1):
                row = gath.at[core, others[i]]
                got(row, s + i)
                go(row, row, f + i, f + i, sibling)

    def from_sibling(c):
        for gath, own, others, peers, s, f, before, fast in gathers(c):
            for i in range(3):
                got(gath.at[1 - core, others[i]], f + i)
            got(gath.at[1 - core, own], f + 3)

    for step, c in (
        (send_pair, 0), (send_pair, 1), (add_cores, 0), (add_cores, 1), (weight_grads, 2), (add_first, 0),
        (add_cores, 2), (add_first, 1), (hit_grads, 0), (add_second, 0), (add_first, 2), (add_second, 1),
        (hit_grads, 1), (pass_row, 0), (add_second, 2), (pass_row, 1), (pass_sibling, 0), (pass_row, 2),
        (pass_sibling, 1), (from_sibling, 0), (attended_products, 0), (pass_sibling, 2), (from_sibling, 1),
        (from_sibling, 2),
    ):
        step(c)
    net.finish()


def final_kernel(queries, grad_out, w_query, gath_a, gath_b, grad_hits_in, layer_in, grad_wo_in, *refs):
    outs, bufs = refs[:7], refs[7:11]
    grad_q, sems = refs[11:]
    grad_queries, grad_wq, grad_wk, grad_wv = bufs
    ready = (layer_in, grad_queries, grad_hits_in, grad_wq, grad_wk, grad_wv, grad_wo_in)
    saves = []

    def save(i):
        c = pltpu.make_async_copy(ready[i], outs[i], sems.at[i])
        c.start()
        saves.append(c)

    for i in (0, 2, 6):
        save(i)

    def blocks(chunk, qb, p):
        core, z = qb // 4, qb % 4
        return gath_a[chunk, core, z, p], gath_b[chunk, core, p, z]

    def place_blocks(chunk, qb, p, out, row):
        for half, block in enumerate(blocks(chunk, qb, p)):
            out[row + half * 64 : row + half * 64 + 64, pair_cols(p)] = block.astype(out.dtype)

    for qb in range(QB):
        for p in range(PAIRS):
            place_blocks(2, qb, p, grad_wk if qb < 4 else grad_wv, (qb % 4) * B)
            place_blocks(1, qb, p, grad_q, qb * B)
        if qb == 3:
            save(4)
    save(5)

    for j in range(2):
        cols = slice(j * 256, j * 256 + 256)
        grad_wq[cols, :] = dot(queries[:, cols], grad_q[...], TN)
    save(3)
    for i in range(4):
        rows = slice(i * 256, i * 256 + 256)
        grad_queries[rows, :] = (grad_out[rows, :].astype(f32) + dot(grad_q[rows, :], w_query[...], NT)).astype(bf16)
    save(1)
    for c in saves:
        c.wait()


def shaped(*shape, dtype=f32):
    return jax.ShapeDtypeStruct(shape, dtype)


VMEM = pl.BlockSpec(memory_space=pltpu.VMEM)
ANY = pl.BlockSpec(memory_space=pl.ANY)
DMA = pltpu.SemaphoreType.DMA


def scratch(*shape, dtype=bf16):
    return pltpu.VMEM(shape, dtype)


def call(kernel, args, outs, scratch_shapes, collective=None, any_in=(), any_out=(), vmem=VMEM_LIMIT, flops=None):
    params = {"vmem_limit_bytes": vmem}
    if collective is not None:
        params |= {"collective_id": collective, "has_side_effects": True}
    return pl.pallas_call(
        kernel,
        out_shape=outs,
        in_specs=[ANY if i in any_in else VMEM for i in range(len(args))],
        out_specs=tuple(ANY if i in any_out else VMEM for i in range(len(outs))),
        scratch_shapes=scratch_shapes,
        compiler_params=pltpu.CompilerParams(**params),
        cost_estimate=flops and pl.CostEstimate(flops=flops, bytes_accessed=4 * MIB, transcendentals=0),
        name=kernel.__name__,
    )(*args)


STAGE_SHAPES = ((3, 4, 4, 64), (3, 3, 4, 64), (3, 3, 4, 64), (3, 4, 64), (3, 3, 64))


def on_device(queries_in, hits_in, w_query, w_key, w_value, w_out, mask_list, grad_out):
    full, weight = scratch(N, D), scratch(D, D)
    turned = scratch(HB, D, B)
    spread = scratch(PAIRS, 2 * B, B)
    lists = [pltpu.SMEM((QB, HB + 1), jnp.int32), pltpu.SMEM((QB,), jnp.int32)]
    q, k, v, natt_e, natt_o, stats_own = call(
        forward_kernel,
        (queries_in, hits_in, w_query, w_key, w_value, grad_out, w_out, mask_list),
        (
            shaped(N, D, dtype=bf16), shaped(N, D, dtype=bf16), shaped(N, D, dtype=bf16),
            shaped(2, 4, 4, 64, B, dtype=bf16), shaped(2, 4, 4, 64, B, dtype=bf16), shaped(QB, 16, B),
        ),
        [
            full, full, weight, weight, weight, full, weight, full, full, full,
            turned, scratch(QB + 1, PAIRS, 2 * B, B), scratch(QB + 1, PAIRS, B, B, dtype=f32),
            scratch(QB + 1, PAIRS, 1, 2 * B, dtype=f32), scratch(QB + 1, PAIRS, 1, 2 * B, dtype=f32),
            scratch(PAIRS, B, 2 * B, dtype=f32), scratch(PAIRS, B, 2 * B, dtype=f32),
            pltpu.SMEM((2, QB * HB + 2), jnp.int32), DMA((7,)), DMA((3,)),
        ],
        any_in=range(7),
        any_out=range(3),
        vmem=FORWARD_LIMIT,
    )
    two = scratch(2, 16, B, dtype=f32)
    three = scratch(3, 2, 16, B, dtype=f32)
    stats, hits_t, gatt = call(
        softmax_kernel,
        (stats_own, hits_in, grad_out, w_out),
        (
            shaped(QB, 16, B), shaped(HB, D, B, dtype=bf16),
            shaped(N, D, dtype=bf16),
        ),
        [
            scratch(4, 16, B, dtype=f32), two, two, three, three, two, two, three, three,
            DMA((14,)), DMA((14,)),
        ],
        collective=0,
        vmem=8 * MIB,
        flops=2 * 10**10,
    )
    even, odd, dkb, dvb = call(
        backward_kernel,
        (q, k, v, gatt, stats, stats_own, natt_e, natt_o, mask_list),
        (
            shaped(2, 2, 4, 4, 64, B, dtype=bf16), shaped(2, 2, 4, 4, 64, B, dtype=bf16),
            shaped(N, D, dtype=bf16), shaped(N, D, dtype=bf16),
        ),
        [
            scratch(N, D, dtype=f32), scratch(N, D, dtype=f32),
            spread, spread, scratch(PAIRS, B, B, dtype=f32),
        ] + lists,
        vmem=20 * MIB,
    )
    stages = [full, scratch(2, 4, 4, 64, B), scratch(2, 4, 4, 64, B)]
    for lead in STAGE_SHAPES:
        stages += [scratch(*lead, B)] * 2
    gath_a, gath_b, grad_hits, layer_out, grad_wo = call(
        total_kernel,
        (even, odd, dkb, dvb, hits_t, w_key, w_value, queries_in, grad_out, w_out),
        (
            shaped(3, 2, 4, 4, 64, B, dtype=bf16), shaped(3, 2, 4, 4, 64, B, dtype=bf16),
            shaped(N, D, dtype=bf16), shaped(N, D, dtype=bf16), shaped(D, D),
        ),
        stages + [DMA((CHUNKS * FLOWS,)), DMA((CHUNKS * FLOWS,))],
        collective=1,
        vmem=20 * MIB,
    )
    square = scratch(D, D, dtype=f32)
    layer_out, grad_queries, grad_hits, grad_wq, grad_wk, grad_wv, grad_wo = call(
        final_kernel,
        (queries_in, grad_out, w_query, gath_a, gath_b, grad_hits, layer_out, grad_wo),
        (
            shaped(N, D, dtype=bf16), shaped(N, D, dtype=bf16), shaped(N, D, dtype=bf16),
            shaped(D, D), shaped(D, D), shaped(D, D), shaped(D, D),
        ),
        [full, square, square, square, full, DMA((7,))],
        any_in=(5, 6, 7),
        any_out=range(7),
        vmem=14 * MIB,
    )
    return (layer_out, grad_queries, grad_hits, grad_wq, grad_wk, grad_wv, grad_wo)


def solution(mesh):
    per_event = P("event", None)
    per_region = P(("event", "region"), None)
    return jax.shard_map(
        on_device,
        mesh=mesh,
        in_specs=(per_event, per_region, P(), P(), P(), P(), per_event, per_event),
        out_specs=(per_event, per_event, per_region, per_event, per_event, per_event, per_event),
        check_vma=False,
    )
```
